32 devices in a mesh: dp: 8 (over z, y), tensor: 4 (over x, core).
Axes of the slice: x: 2, y: 2, z: 4, core: 2. Of those that a mesh axis runs over, the one named last changes fastest.
Arguments:
- tokens: bfloat16 [18464, 1024], P(('dp', 'tensor')), may hold values from -6 to 6
- cotangent: bfloat16 [18464, 1024], P(('dp', 'tensor')), may hold values from -6 to 6
- image_mask: int32 [32], P('dp'), may hold values 0 or 1
- query_weight: float32 [1024, 1024], P('dp', 'tensor'), may hold values from -0.1875 to 0.1875
- key_weight: float32 [1024, 1024], P('dp', 'tensor'), may hold values from -0.1875 to 0.1875
- value_weight: float32 [1024, 1024], P('dp', 'tensor'), may hold values from -0.1875 to 0.1875
- out_weight: float32 [1024, 1024], P('tensor', 'dp'), may hold values from -1 to 1
- up_weight: float32 [1024, 4096], P('dp', 'tensor'), may hold values from -0.1875 to 0.1875
- down_weight: float32 [4096, 1024], P('tensor', 'dp'), may hold values from -0.1875 to 0.1875
- query_bias: float32 [16, 64], P('tensor', 'dp'), may hold values from -3 to 3
- value_bias: float32 [16, 64], P('tensor', 'dp'), may hold values from -3 to 3
- up_bias: float32 [32, 128], P('tensor', 'dp'), may hold values from -3 to 3
- attn_gain: float32 [1024], P('dp'), may hold values from 0.1 to 1.9
- attn_shift: float32 [1024], P('dp'), may hold values from -3 to 3
- mlp_gain: float32 [1024], P('dp'), may hold values from 0.1 to 1.9
- mlp_shift: float32 [1024], P('dp'), may hold values from -3 to 3
- out_bias: float32 [1024], P('dp'), may hold values from -3 to 3
- down_bias: float32 [1024], P('dp'), may hold values from -3 to 3
Outputs:
- block_out: bfloat16 [18464, 1024], P(('dp', 'tensor'))
- tokens_grad: float32 [18464, 1024], P(('dp', 'tensor'))
- query_weight_grad: float32 [1024, 1024], P('dp', 'tensor')
- key_weight_grad: float32 [1024, 1024], P('dp', 'tensor')
- value_weight_grad: float32 [1024, 1024], P('dp', 'tensor')
- out_weight_grad: float32 [1024, 1024], P('tensor', 'dp')
- up_weight_grad: float32 [1024, 4096], P('dp', 'tensor')
- down_weight_grad: float32 [4096, 1024], P('tensor', 'dp')
- query_bias_grad: float32 [16, 64], P('tensor', 'dp')
- value_bias_grad: float32 [16, 64], P('tensor', 'dp')
- up_bias_grad: float32 [32, 128], P('tensor', 'dp')
- attn_gain_grad: float32 [1024], P('dp')
- attn_shift_grad: float32 [1024], P('dp')
- mlp_gain_grad: float32 [1024], P('dp')
- mlp_shift_grad: float32 [1024], P('dp')
- out_bias_grad: float32 [1024], P('dp')
- down_bias_grad: float32 [1024], P('dp')
The draws below stay inside these ranges and needn't reach their ends.
All inputs are finite; a program needn't handle non-finite values. No bound on the sum of `image_mask` on one device may be relied on, other than what follows from the above.
Results may differ from the reference program's by a relative error of at most 0.018.
Values may be sent and summed in bfloat16 or wider, within the bound.
A program may use at most 192 MiB of HBM per device.

```python
import math
import jax
import jax.numpy as jnp
from jax import lax

D = 1024
H = 16
HD = 64
FF = 4096
SEQ = 577
IMG = 4
IMAGES = 32
TOKENS = 18464


def set_ends(values, rng, low, largest):
    index_at = [jax.random.randint(jax.random.fold_in(rng, axis), (), 0, length) for axis, length in enumerate(values.shape)]
    main_axis = values.shape.index(max(values.shape))
    next_to = index_at[:main_axis] + [(index_at[main_axis] + 1) % values.shape[main_axis]] + index_at[main_axis + 1:]
    return values.at[tuple(index_at)].set(low).at[tuple(next_to)].set(largest)


def levels(key, dims, shards, least, high):
    loudness, own = 1.0, jax.random.fold_in(key, 6)
    for axis_at, parts in shards:
        draws = jnp.exp(jax.random.uniform(jax.random.fold_in(own, axis_at), (parts,), jnp.float32, least / len(shards), high / len(shards)))
        loudness = loudness * jnp.repeat(draws, dims[axis_at] // parts).reshape([-1 if axis == axis_at else 1 for axis in range(len(dims))])
    return loudness


def bell_draw(rng, shape, spread, reach, shards=(), kind=jnp.bfloat16):
    values = jax.random.normal(rng, shape, jnp.float32) * spread
    if len(shards) > 0:
        values = levels(rng, shape, shards, -0.22, 0.18) * values
    return jnp.clip(values, min=-reach, max=reach).astype(kind)


def setup_inputs(seed: int = 0) -> dict:
    key_of = jax.random.split(jax.random.key(seed), 19)
    return {
        "tokens": bell_draw(key_of[0], (TOKENS, D), 1.0, 6.0, ((0, 32),)),
        "cotangent": bell_draw(key_of[1], (TOKENS, D), 1.0, 6.0, ((0, 32),)),
        "image_mask": set_ends((jax.random.randint(key_of[2], (IMAGES,), 0, 4) < 3).astype(jnp.int32), jax.random.fold_in(key_of[2], 1), 0, 1),
        "query_weight": bell_draw(key_of[3], (D, D), D ** -0.5, 0.1875, ((0, 8), (1, 4)), jnp.float32),
        "key_weight": bell_draw(key_of[4], (D, D), D ** -0.5, 0.1875, ((0, 8), (1, 4)), jnp.float32),
        "value_weight": bell_draw(key_of[5], (D, D), D ** -0.5, 0.1875, ((0, 8), (1, 4)), jnp.float32),
        "out_weight": bell_draw(key_of[6], (D, D), (D // 32) ** -0.5, 1.0, ((0, 4), (1, 8)), jnp.float32),
        "up_weight": bell_draw(key_of[7], (D, FF), D ** -0.5, 0.1875, ((0, 8), (1, 4)), jnp.float32),
        "down_weight": bell_draw(key_of[8], (FF, D), (FF // 4) ** -0.5, 0.1875, ((0, 4), (1, 8)), jnp.float32),
        "query_bias": bell_draw(key_of[9], (H, HD), 0.5, 3.0, ((0, 4), (1, 8)), jnp.float32),
        "value_bias": bell_draw(key_of[10], (H, HD), 0.5, 3.0, ((0, 4), (1, 8)), jnp.float32),
        "up_bias": bell_draw(key_of[11], (FF // 128, 128), 0.5, 3.0, ((0, 4), (1, 8)), jnp.float32),
        "attn_gain": jnp.clip(1.0 + 0.18 * jax.random.normal(key_of[12], (D,), jnp.float32), 0.1, 1.9),
        "attn_shift": bell_draw(key_of[13], (D,), 0.5, 3.0, ((0, 8),), jnp.float32),
        "mlp_gain": jnp.clip(1.0 + 0.18 * jax.random.normal(key_of[14], (D,), jnp.float32), 0.1, 1.9),
        "mlp_shift": bell_draw(key_of[15], (D,), 0.5, 3.0, ((0, 8),), jnp.float32),
        "out_bias": bell_draw(key_of[16], (D,), 0.5, 3.0, ((0, 8),), jnp.float32),
        "down_bias": bell_draw(key_of[17], (D,), 0.5, 3.0, ((0, 8),), jnp.float32),
    }


EPS = 1e-05
SLOPE = 1.702
HIGH = lax.Precision.HIGHEST

@jax.custom_vjp
def low(v):
    return lax.optimization_barrier(v.astype(jnp.bfloat16)).astype(jnp.float32)

@jax.custom_vjp
def low_back(v):
    return v

def low_keep(v):
    return (low(v), None)

def low_pass(kept, grad):
    return (grad,)

def back_keep(v):
    return (v, None)

def back_low(kept, grad):
    return (low(grad),)
low.defvjp(low_keep, low_pass)
low_back.defvjp(back_keep, back_low)

def both_ways(values):
    return low(low_back(values))

def product(left, right):
    return jnp.dot(left, right, precision=HIGH, preferred_element_type=jnp.float32)

def normalize(values, gain, shift):
    centre = values - lax.optimization_barrier(jnp.mean(values, axis=-1, keepdims=True))
    inverse = lax.rsqrt(lax.optimization_barrier(jnp.mean(centre * centre, axis=-1, keepdims=True)) + EPS)
    return centre * inverse * gain + shift

def attend(pieces):
    query, key, value = pieces
    scale = 1.0 / math.sqrt(HD)
    scores = low_back(jnp.einsum('qhd,khd->hqk', query, key, precision=HIGH) * scale)
    probs = jax.nn.softmax(scores, axis=-1)
    return jnp.einsum('hqk,khd->qhd', low(probs), value, precision=HIGH)

def block(params, inputs, row_mask):
    rounded = tuple((low(item) for item in params))
    w_query, w_key, w_value, w_out, w_up, w_down, b_query, b_value, b_up, g_attn, s_attn, g_mlp, s_mlp, b_out, b_down = rounded
    normed_a = low(normalize(inputs, g_attn, s_attn))
    query = both_ways(product(normed_a, w_query) + b_query.reshape(-1))
    key = both_ways(product(normed_a, w_key))
    value = both_ways(product(normed_a, w_value) + b_value.reshape(-1))
    images = inputs.shape[0] // SEQ
    shaped = (images, SEQ, H, HD)
    mixed = lax.map(jax.checkpoint(attend), (query.reshape(shaped), key.reshape(shaped), value.reshape(shaped)))
    mixed = both_ways(mixed.reshape(-1, D))
    middle = inputs + low_back(product(mixed, w_out)) + b_out
    normed_m = low(normalize(middle, g_mlp, s_mlp))
    pre = low_back(product(normed_m, w_up) + b_up.reshape(-1))
    hidden = low(pre * jax.nn.sigmoid(SLOPE * pre))
    result = middle + low_back(product(hidden, w_down)) + b_down
    return result * row_mask[:, None]

def reference(tokens, cotangent, image_mask, query_weight, key_weight, value_weight, out_weight, up_weight, down_weight, query_bias, value_bias, up_bias, attn_gain, attn_shift, mlp_gain, mlp_shift, out_bias, down_bias):
    params = (query_weight, key_weight, value_weight, out_weight, up_weight, down_weight, query_bias, value_bias, up_bias, attn_gain, attn_shift, mlp_gain, mlp_shift, out_bias, down_bias)
    params = tuple((item.astype(jnp.float32) for item in params))
    groups = IMAGES // IMG
    inputs = tokens.astype(jnp.float32).reshape(groups, IMG * SEQ, D)
    grads_in = cotangent.astype(jnp.float32).reshape(groups, IMG * SEQ, D)
    masks = jnp.repeat(image_mask.astype(jnp.float32), SEQ).reshape(groups, IMG * SEQ)

    def step(totals, batch):
        values, grad_values, mask_rows = batch
        result, pull = jax.vjp(lambda prm, inp: block(prm, inp, mask_rows), params, values)
        param_grads, input_grad = pull(grad_values)
        totals = jax.tree.map(lambda left, right: left + right, totals, param_grads)
        return (totals, (result.astype(jnp.bfloat16), input_grad))
    zeros = tuple((jnp.zeros_like(item) for item in params))
    totals, (outputs, input_grads) = lax.scan(step, zeros, (inputs, grads_in, masks))
    return (outputs.reshape(TOKENS, D), input_grads.reshape(TOKENS, D), totals[0], totals[1], totals[2], totals[3], totals[4], totals[5], totals[6], totals[7], totals[8], totals[9], totals[10], totals[11], totals[12], totals[13], totals[14])
```

```python
import functools
import math

import jax
import jax.numpy as jnp
from jax import lax
from jax.experimental import pallas as pl
from jax.experimental.pallas import tpu as pltpu
from jax.sharding import PartitionSpec as P

HD = 64
EPS = 1e-05
SLOPE = 1.702
MESH = pl.DeviceIdType.MESH
BF = jnp.bfloat16
F32 = jnp.float32


def coords(zs):
    dp, tn = lax.axis_index("dp"), lax.axis_index("tensor")
    z, y = dp // 2, dp % 2
    x, c = tn // 2, tn % 2
    over_y = (dp + 1 - 2 * y, tn)
    over_x = (dp, tn + 2 - 4 * x)
    first = (dp + (1 - c) * (1 - 2 * y), tn + c * (2 - 4 * x))
    second = (dp + c * (1 - 2 * y), tn + (1 - c) * (2 - 4 * x))
    sibling = (dp, tn + 1 - 2 * c)
    del over_y, over_x
    fx, fy = x + c * (1 - 2 * x), y + (1 - c) * (1 - 2 * y)
    sx, sy = x + (1 - c) * (1 - 2 * x), y + c * (1 - 2 * y)
    return dict(
        dp=dp, tn=tn, z=z, y=y, x=x, c=c, first=first, second=second, sibling=sibling,
        fx=fx, fy=fy, sx=sx, sy=sy, zs=zs,
    )


def z_peer(at, step):
    return (lax.rem(at["z"] + step, at["zs"]) * 2 + at["y"], at["tn"])


def enter(at):
    barrier = pltpu.get_barrier_semaphore()
    peers = [at["first"], at["second"], at["sibling"]]
    for peer in peers:
        pl.semaphore_signal(barrier, inc=1, device_id=peer, device_id_type=MESH)

    @pl.loop(1, at["zs"])
    def _(step):
        pl.semaphore_signal(barrier, inc=1, device_id=z_peer(at, step), device_id_type=MESH)

    pl.semaphore_wait(barrier, len(peers) + at["zs"] - 1)


def remote(src, dst, send, recv, peer):
    return pltpu.make_async_remote_copy(
        src_ref=src, dst_ref=dst, send_sem=send, recv_sem=recv, device_id=peer, device_id_type=MESH
    )


class Gather:
    def __init__(self, at, own, bufs, local, zsend, zrecv, psend, precv):
        self.at, self.own, self.bufs = at, own, bufs
        self.local, self.zsend, self.zrecv, self.psend, self.precv = local, zsend, zrecv, psend, precv

    def line(self, k, x, c, y):
        return self.bufs[k].at[x, c, :, y]

    def place(self, k):
        at = self.at
        return pltpu.make_async_copy(
            self.own[k], self.bufs[k].at[at["x"], at["c"], at["z"], at["y"]], self.local.at[k]
        )

    def along_z(self, k, step, source):
        at = self.at
        return remote(
            self.own[k],
            self.bufs[k].at[at["x"], at["c"], source, at["y"]],
            self.zsend.at[k, step],
            self.zrecv.at[k, step],
            z_peer(at, step),
        )

    def to(self, k, kind):
        at = self.at
        x, y, c = at["x"], at["y"], at["c"]
        lines = [(x, y), (x, y), (at["fx"], at["fy"]), (x, y), (at["fx"], at["fy"]), (at["sx"], at["sy"]), (1 - x, 1 - y)]
        peer = [at["first"], at["second"], at["second"]] + [at["sibling"]] * 4
        lx, ly = lines[kind]
        ref = self.line(k, lx, c, ly)
        return remote(ref, ref, self.psend.at[k, kind], self.precv.at[k, kind], peer[kind])

    def start(self, k):
        self.place(k).start()

        @pl.loop(1, self.at["zs"])
        def _(step):
            self.along_z(k, step, self.at["z"]).start()

    def after_z(self, k):
        at = self.at
        self.place(k).wait()

        @pl.loop(1, at["zs"])
        def _(step):
            self.along_z(k, step, lax.rem(at["z"] - step + at["zs"], at["zs"])).wait_recv()

        for kind in (0, 1, 3):
            self.to(k, kind).start()

    def wait(self, k, kind):
        at = self.at
        ref = self.line(k, at["x"], at["c"], at["y"])
        x, y, c = at["x"], at["y"], at["c"]
        got = [
            (at["fx"], c, at["fy"]),
            (at["sx"], c, at["sy"]),
            (1 - x, c, 1 - y),
            (x, 1 - c, y),
            (at["sx"], 1 - c, at["sy"]),
            (at["fx"], 1 - c, at["fy"]),
            (1 - x, 1 - c, 1 - y),
        ][kind]
        ref = self.line(k, *got)
        remote(ref, ref, self.psend.at[k, kind], self.precv.at[k, kind], at["sibling"]).wait_recv()

    def after_first(self, k):
        self.wait(k, 0)
        self.to(k, 2).start()
        self.to(k, 4).start()

    def after_second(self, k):
        self.wait(k, 1)
        self.to(k, 5).start()
        self.wait(k, 2)
        self.to(k, 6).start()

    def done(self, k):
        for kind in (3, 4, 5, 6):
            self.wait(k, kind)

    def drain(self, k):
        @pl.loop(1, self.at["zs"])
        def _(step):
            self.along_z(k, step, self.at["z"]).wait_send()

        for kind in range(7):
            self.to(k, kind).wait_send()


def gather_kernel(n, zs, *refs):
    own, bufs, sems = refs[:n], refs[n : 2 * n], refs[2 * n :]
    at = coords(zs)
    enter(at)
    g = Gather(at, own, bufs, *sems)
    for k in range(n):
        g.start(k)
    for k in range(n + 2):
        if k < n:
            g.after_z(k)
        if 0 <= k - 1 < n:
            g.after_first(k - 1)
        if 0 <= k - 2 < n:
            g.after_second(k - 2)
    for k in range(n):
        g.done(k)
    for k in range(n):
        g.drain(k)


def gather(own, zs):
    n = len(own)
    return pl.pallas_call(
        functools.partial(gather_kernel, n, zs),
        out_shape=[jax.ShapeDtypeStruct((2, 2, zs, 2) + b.shape, b.dtype) for b in own],
        in_specs=[pl.BlockSpec(memory_space=pl.ANY)] * n,
        out_specs=[pl.BlockSpec(memory_space=pl.ANY)] * n,
        scratch_shapes=[
            pltpu.SemaphoreType.DMA((n,)),
            pltpu.SemaphoreType.DMA((n, zs)),
            pltpu.SemaphoreType.DMA((n, zs)),
            pltpu.SemaphoreType.DMA((n, 7)),
            pltpu.SemaphoreType.DMA((n, 7)),
        ],
        compiler_params=pltpu.CompilerParams(collective_id=0, has_side_effects=True),
        name="gather_weights",
    )(*own)


def scatter_kernel(n, zs, *refs):
    parts, outs = refs[:n], refs[n : 2 * n]
    refs = refs[2 * n :]
    kept, rc, rs, rz = refs[:n], refs[n : 2 * n], refs[2 * n : 3 * n], refs[3 * n : 4 * n]
    local, zsend, zrecv, psend, precv = refs[4 * n :]
    at = coords(zs)
    x, y, c, z = at["x"], at["y"], at["c"], at["z"]
    enter(at)

    def keep(k):
        return pltpu.make_async_copy(parts[k].at[:, c], kept[k], local.at[k])

    def to_sibling(k):
        return remote(parts[k].at[:, 1 - c], rc[k], psend.at[k, 0], precv.at[k, 0], at["sibling"])

    def to_second(k, which):
        lx, ly = ((at["sx"], at["sy"]), (1 - x, 1 - y))[which]
        return remote(
            kept[k].at[lx, :, ly], rs[k].at[which], psend.at[k, 1 + which], precv.at[k, 1 + which], at["second"]
        )

    def to_first(k):
        return remote(kept[k].at[at["fx"], :, at["fy"]], rs[k].at[2], psend.at[k, 3], precv.at[k, 3], at["first"])

    def along_z(k, step):
        return remote(
            kept[k].at[x, lax.rem(z + step, zs), y], rz[k].at[step], zsend.at[k, step], zrecv.at[k, step], z_peer(at, step)
        )

    def add(dst, src):
        dst[...] = (dst[...].astype(F32) + src[...].astype(F32)).astype(dst.dtype)

    def stage0(k):
        to_sibling(k).start()
        keep(k).start()

    def stage1(k):
        to_sibling(k).wait_recv()
        keep(k).wait()

        for which, (lx, ly) in enumerate(
            ((1 - x, 1 - y), (at["sx"], at["sy"]), (at["fx"], at["fy"]), (x, y))
        ):

            @pl.loop(0, zs)
            def _(i):
                add(kept[k].at[lx, i, ly], rc[k].at[lx, i, ly])

            if which == 0:
                to_second(k, 1).start()
            elif which == 1:
                to_second(k, 0).start()

    def stage2(k):
        to_second(k, 1).wait_recv()

        @pl.loop(0, zs)
        def _(i):
            add(kept[k].at[at["fx"], i, at["fy"]], rs[k].at[1, i])

        to_first(k).start()
        to_second(k, 0).wait_recv()

        @pl.loop(0, zs)
        def _(i):
            add(kept[k].at[x, i, y], rs[k].at[0, i])

    def stage3(k):
        to_first(k).wait_recv()

        @pl.loop(0, zs)
        def _(i):
            add(kept[k].at[x, i, y], rs[k].at[2, i])

        @pl.loop(1, zs)
        def _(step):
            along_z(k, step).start()

    def stage4(k):
        outs[k][...] = kept[k][x, z, y].astype(F32)

        @pl.loop(1, zs)
        def _(step):
            along_z(k, step).wait_recv()
            outs[k][...] += rz[k][step].astype(F32)

    stages = (stage0, stage1, stage2, stage3, stage4)
    for tick in range(n + len(stages) - 1):
        for late, stage in enumerate(stages):
            if 0 <= tick - late < n:
                stage(tick - late)
    for k in range(n):
        to_sibling(k).wait_send()
        to_second(k, 0).wait_send()
        to_second(k, 1).wait_send()
        to_first(k).wait_send()

        @pl.loop(1, zs)
        def _(step):
            along_z(k, step).wait_send()


def scatter(parts, zs):
    n = len(parts)
    blocks = [p.shape[4:] for p in parts]
    return pl.pallas_call(
        functools.partial(scatter_kernel, n, zs),
        out_shape=[jax.ShapeDtypeStruct(b, F32) for b in blocks],
        in_specs=[pl.BlockSpec(memory_space=pl.ANY)] * n,
        out_specs=[pl.BlockSpec(memory_space=pltpu.VMEM)] * n,
        scratch_shapes=[pltpu.VMEM((2, zs, 2) + b, p.dtype) for b, p in zip(blocks, parts)]
        + [pltpu.VMEM((2, zs, 2) + b, p.dtype) for b, p in zip(blocks, parts)]
        + [pltpu.VMEM((3, zs) + b, p.dtype) for b, p in zip(blocks, parts)]
        + [pltpu.VMEM((zs,) + b, p.dtype) for b, p in zip(blocks, parts)]
        + [
            pltpu.SemaphoreType.DMA((n,)),
            pltpu.SemaphoreType.DMA((n, zs)),
            pltpu.SemaphoreType.DMA((n, zs)),
            pltpu.SemaphoreType.DMA((n, 4)),
            pltpu.SemaphoreType.DMA((n, 4)),
        ],
        compiler_params=pltpu.CompilerParams(
            collective_id=1, has_side_effects=True, vmem_limit_bytes=52 * 1024 * 1024
        ),
        name="scatter_grads",
    )(*parts)


def normalize(values, gain, shift):
    centre = values - jnp.mean(values, axis=-1, keepdims=True)
    inverse = lax.rsqrt(jnp.mean(centre * centre, axis=-1, keepdims=True) + EPS)
    normed = centre * inverse
    return (normed * gain + shift, normed, inverse)


def normalize_back(grad_out, normed, inverse, gain):
    scaled = grad_out * gain
    grad_in = inverse * (
        scaled
        - jnp.mean(scaled, axis=-1, keepdims=True)
        - normed * jnp.mean(scaled * normed, axis=-1, keepdims=True)
    )
    return (grad_in, jnp.sum(grad_out * normed, axis=0), jnp.sum(grad_out, axis=0))


def attend(query, key, value):
    scale = 1.0 / math.sqrt(query.shape[-1])
    scores = jnp.einsum("qhd,khd->hqk", query, key, preferred_element_type=F32) * scale
    highest = jnp.max(scores, axis=-1, keepdims=True)
    expo = jnp.exp(scores - highest)
    total = jnp.sum(expo, axis=-1, keepdims=True)
    probs = (expo / total).astype(BF)
    mixed = jnp.einsum("hqk,khd->qhd", probs, value, preferred_element_type=F32)
    return (mixed.astype(BF), (highest + jnp.log(total))[..., 0])


def attend_back(query, key, value, grad_mixed, log_total):
    scale = 1.0 / math.sqrt(query.shape[-1])
    scores = jnp.einsum("qhd,khd->hqk", query, key, preferred_element_type=F32) * scale
    probs = jnp.exp(scores - log_total[..., None])
    grad_value = jnp.einsum(
        "hqk,qhd->khd", probs.astype(BF), grad_mixed, preferred_element_type=F32
    ).astype(BF)
    grad_probs = jnp.einsum("qhd,khd->hqk", grad_mixed, value, preferred_element_type=F32)
    grad_scores = probs * (grad_probs - jnp.sum(grad_probs * probs, axis=-1, keepdims=True))
    grad_scores = grad_scores.astype(BF)
    grad_query = jnp.einsum("hqk,khd->qhd", grad_scores, key, preferred_element_type=F32) * scale
    grad_key = jnp.einsum("hqk,qhd->khd", grad_scores, query, preferred_element_type=F32) * scale
    return (grad_query.astype(BF), grad_key.astype(BF), grad_value)


def on_device(
    tokens,
    cotangent,
    image_mask,
    query_weight,
    key_weight,
    value_weight,
    out_weight,
    up_weight,
    down_weight,
    query_bias,
    value_bias,
    up_bias,
    attn_gain,
    attn_shift,
    mlp_gain,
    mlp_shift,
    out_bias,
    down_bias,
):
    rows, dim = tokens.shape
    dps, tns = lax.axis_size("dp"), lax.axis_size("tensor")
    zs = dps // 2
    hw = query_weight.shape[1]
    half = up_weight.shape[1] // 2
    low_up, low_down = up_weight.astype(BF), down_weight.astype(BF).T
    small = jnp.concatenate(
        [query_bias.reshape(-1), value_bias.reshape(-1), up_bias.reshape(-1)]
        + [attn_gain, attn_shift, mlp_gain, mlp_shift, out_bias, down_bias]
    ).astype(BF)
    n_small = small.shape[0]
    pad = -(-n_small // 2048) * 2048
    own = [
        jnp.pad(small, (0, pad - n_small)).reshape(-1, 128),
        jnp.concatenate([query_weight.astype(BF), key_weight.astype(BF)], axis=1),
        jnp.concatenate([value_weight.astype(BF), out_weight.astype(BF).T], axis=1),
        low_up[:, :half],
        low_up[:, half:],
        low_down[:, :half],
        low_down[:, half:],
    ]
    got = gather(own, zs)
    vecs = got[0].reshape(tns, dps, pad).astype(F32)
    heads_t = query_bias.shape[0]
    q_b, v_b, u_b = query_bias.size, value_bias.size, up_bias.size
    vec_query = vecs[:, :, :q_b].reshape(tns, dps, heads_t, -1).transpose(0, 2, 1, 3).reshape(-1)
    vec_value = vecs[:, :, q_b : q_b + v_b].reshape(tns, dps, heads_t, -1).transpose(0, 2, 1, 3).reshape(-1)
    at_u = q_b + v_b
    vec_up = (
        vecs[:, :, at_u : at_u + u_b].reshape(tns, dps, up_bias.shape[0], -1).transpose(0, 2, 1, 3).reshape(-1)
    )
    at_d = at_u + u_b
    own_d = attn_gain.shape[0]
    gain_a, shift_a, gain_m, shift_m, vec_out, vec_down = (
        vecs[0, :, at_d + i * own_d : at_d + (i + 1) * own_d].reshape(-1) for i in range(6)
    )
    mats = [g.reshape(tns, dim, -1) for g in got[1:]]

    def whole(pieces):
        return jnp.concatenate(pieces, axis=2).transpose(1, 0, 2).reshape(dim, -1)

    full_query, full_key = whole([mats[0][:, :, :hw]]), whole([mats[0][:, :, hw:]])
    full_value, full_out_t = whole([mats[1][:, :, :hw]]), whole([mats[1][:, :, hw:]])
    whole_up, whole_down_t = whole(mats[2:4]), whole(mats[4:6])

    image = lax.axis_index("tensor")
    row_mask = image_mask[image].astype(F32)
    inputs = tokens.astype(F32)
    normed_a, unit_a, inverse_a = normalize(inputs, gain_a, shift_a)
    attn_in = normed_a.astype(BF)
    query = (jnp.dot(attn_in, full_query, preferred_element_type=F32) + vec_query).astype(BF)
    key = jnp.dot(attn_in, full_key, preferred_element_type=F32).astype(BF)
    value = (jnp.dot(attn_in, full_value, preferred_element_type=F32) + vec_value).astype(BF)
    shaped = (rows, -1, HD)
    q3, k3, v3 = query.reshape(shaped), key.reshape(shaped), value.reshape(shaped)
    mixed3, log_total = attend(q3, k3, v3)
    mixed = mixed3.reshape(rows, dim)
    middle = inputs + jnp.einsum("rh,dh->rd", mixed, full_out_t, preferred_element_type=F32) + vec_out
    normed_m, unit_m, inverse_m = normalize(middle, gain_m, shift_m)
    grad_out = cotangent.astype(F32) * row_mask
    grad_down_b = jnp.sum(grad_out, axis=0)
    mlp_in = normed_m.astype(BF)
    pre = jnp.dot(mlp_in, whole_up, preferred_element_type=F32) + vec_up
    sigma = jax.nn.sigmoid(SLOPE * pre)
    hidden = (pre * sigma).astype(BF)
    branch = jnp.einsum("rf,df->rd", hidden, whole_down_t, preferred_element_type=F32)
    block_out = ((middle + branch + vec_down) * row_mask).astype(BF)
    grad_branch = grad_out.astype(BF)
    down_t_grad = jnp.einsum("rd,rf->df", grad_branch, hidden, preferred_element_type=F32).astype(BF)
    grad_hidden = jnp.dot(grad_branch, whole_down_t, preferred_element_type=F32)
    grad_pre = (grad_hidden * (sigma + SLOPE * pre * sigma * (1.0 - sigma))).astype(BF)
    up_b_grad = jnp.sum(grad_pre.astype(F32), axis=0)
    up_grad = jnp.einsum("rd,rf->df", mlp_in, grad_pre, preferred_element_type=F32).astype(BF)
    grad_normed_m = jnp.einsum("rf,df->rd", grad_pre, whole_up, preferred_element_type=F32)
    grad_mid_norm, grad_gain_m, grad_shift_m = normalize_back(grad_normed_m, unit_m, inverse_m, gain_m)
    grad_middle = grad_out + grad_mid_norm
    grad_out_b = jnp.sum(grad_middle, axis=0)
    grad_attn = grad_middle.astype(BF)
    out_t_grad = jnp.einsum("rd,rh->dh", grad_attn, mixed, preferred_element_type=F32).astype(BF)
    grad_mixed = jnp.dot(grad_attn, full_out_t, preferred_element_type=F32).astype(BF)
    gq3, gk3, gv3 = attend_back(q3, k3, v3, grad_mixed.reshape(shaped), log_total)
    grad_query, grad_key, grad_value = gq3.reshape(rows, dim), gk3.reshape(rows, dim), gv3.reshape(rows, dim)
    query_grad = jnp.einsum("rd,rh->dh", attn_in, grad_query, preferred_element_type=F32).astype(BF)
    key_grad = jnp.einsum("rd,rh->dh", attn_in, grad_key, preferred_element_type=F32).astype(BF)
    value_grad = jnp.einsum("rd,rh->dh", attn_in, grad_value, preferred_element_type=F32).astype(BF)
    query_b_grad = jnp.sum(grad_query.astype(F32), axis=0)
    value_b_grad = jnp.sum(grad_value.astype(F32), axis=0)
    grad_normed_a = (
        jnp.einsum("rh,dh->rd", grad_query, full_query, preferred_element_type=F32)
        + jnp.einsum("rh,dh->rd", grad_key, full_key, preferred_element_type=F32)
        + jnp.einsum("rh,dh->rd", grad_value, full_value, preferred_element_type=F32)
    )
    grad_in_norm, grad_gain_a, grad_shift_a = normalize_back(grad_normed_a, unit_a, inverse_a, gain_a)
    tokens_grad = grad_middle + grad_in_norm

    def blocks(mat):
        return mat.reshape(dim, tns, -1).transpose(1, 0, 2)

    def frame(mat, width):
        return mat.reshape(2, 2, zs, 2, -1, width)

    def spread(vec, lead):
        return vec.reshape(tns, lead, dps, -1).transpose(0, 2, 1, 3).reshape(tns, dps, -1)

    small_d = jnp.concatenate(
        [
            v.reshape(dps, -1)
            for v in (grad_gain_a, grad_shift_a, grad_gain_m, grad_shift_m, grad_out_b, grad_down_b)
        ],
        axis=1,
    )
    small_grad = jnp.concatenate(
        [
            spread(query_b_grad, heads_t),
            spread(value_b_grad, heads_t),
            spread(up_b_grad, up_bias.shape[0]),
            jnp.broadcast_to(small_d, (tns,) + small_d.shape),
        ],
        axis=2,
    )
    small_grad = jnp.pad(small_grad, ((0, 0), (0, 0), (0, pad - n_small)))
    up_blocks, down_blocks = blocks(up_grad), blocks(down_t_grad)
    parts = [
        frame(down_blocks[:, :, :half], half),
        frame(down_blocks[:, :, half:], half),
        frame(up_blocks[:, :, :half], half),
        frame(up_blocks[:, :, half:], half),
        frame(jnp.concatenate([blocks(value_grad), blocks(out_t_grad)], axis=2), 2 * hw),
        frame(jnp.concatenate([blocks(query_grad), blocks(key_grad)], axis=2), 2 * hw),
        frame(small_grad, 128),
    ]
    down0, down1, up0, up1, vo, qk, sm = scatter(parts, zs)
    sm = sm.reshape(-1)
    return (
        block_out,
        tokens_grad,
        qk[:, :hw],
        qk[:, hw:],
        vo[:, :hw],
        vo[:, hw:].T,
        jnp.concatenate([up0, up1], axis=1),
        jnp.concatenate([down0, down1], axis=1).T,
        sm[:q_b].reshape(query_bias.shape),
        sm[q_b : q_b + v_b].reshape(value_bias.shape),
        sm[at_u : at_u + u_b].reshape(up_bias.shape),
    ) + tuple(sm[at_d + i * own_d : at_d + (i + 1) * own_d] for i in range(6))


def solution(mesh):
    wide, tall = P("dp", "tensor"), P("tensor", "dp")
    rows = P(("dp", "tensor"), None)
    weights = (wide, wide, wide, tall, wide, tall, tall, tall, tall)
    vectors = (P("dp"),) * 6
    return jax.shard_map(
        on_device,
        mesh=mesh,
        in_specs=(rows, rows, P("dp")) + weights + vectors,
        out_specs=(rows, rows) + weights + vectors,
        check_vma=False,
    )
```

```python
import functools
import math

import jax
import jax.numpy as jnp
from jax import lax
from jax.experimental import pallas as pl
from jax.experimental.pallas import tpu as pltpu
from jax.sharding import PartitionSpec as P

HD = 64
EPS = 1e-05
SLOPE = 1.702
MESH = pl.DeviceIdType.MESH
BF = jnp.bfloat16
F32 = jnp.float32


def coords(zs):
    dp, tn = lax.axis_index("dp"), lax.axis_index("tensor")
    z, y = dp // 2, dp % 2
    x, c = tn // 2, tn % 2
    over_y = (dp + 1 - 2 * y, tn)
    over_x = (dp, tn + 2 - 4 * x)
    first = (dp + (1 - c) * (1 - 2 * y), tn + c * (2 - 4 * x))
    second = (dp + c * (1 - 2 * y), tn + (1 - c) * (2 - 4 * x))
    sibling = (dp, tn + 1 - 2 * c)
    del over_y, over_x
    fx, fy = x + c * (1 - 2 * x), y + (1 - c) * (1 - 2 * y)
    sx, sy = x + (1 - c) * (1 - 2 * x), y + c * (1 - 2 * y)
    return dict(
        dp=dp, tn=tn, z=z, y=y, x=x, c=c, first=first, second=second, sibling=sibling,
        fx=fx, fy=fy, sx=sx, sy=sy, zs=zs,
    )


def z_peer(at, step):
    return (lax.rem(at["z"] + step, at["zs"]) * 2 + at["y"], at["tn"])


def enter(at):
    barrier = pltpu.get_barrier_semaphore()
    peers = [at["first"], at["second"], at["sibling"]]
    for peer in peers:
        pl.semaphore_signal(barrier, inc=1, device_id=peer, device_id_type=MESH)

    @pl.loop(1, at["zs"])
    def _(step):
        pl.semaphore_signal(barrier, inc=1, device_id=z_peer(at, step), device_id_type=MESH)

    pl.semaphore_wait(barrier, len(peers) + at["zs"] - 1)


def remote(src, dst, send, recv, peer):
    return pltpu.make_async_remote_copy(
        src_ref=src, dst_ref=dst, send_sem=send, recv_sem=recv, device_id=peer, device_id_type=MESH
    )


class Gather:
    def __init__(self, at, own, bufs, sems):
        self.at, self.own, self.bufs = at, own, bufs
        (self.local, self.zsend, self.zrecv, self.fsend, self.frecv, self.ssend, self.srecv, self.psend, self.precv) = sems

    def place(self, k):
        at = self.at
        return pltpu.make_async_copy(
            self.own[k], self.bufs[k].at[at["x"], at["c"], at["z"], at["y"]], self.local.at[k]
        )

    def source(self, step):
        at = self.at
        return lax.rem(at["z"] - step + at["zs"], at["zs"])

    def along_z(self, k, step, z):
        at = self.at
        dst = self.bufs[k].at[at["x"], at["c"], z, at["y"]]
        return remote(self.own[k], dst, self.zsend.at[k, step], self.zrecv.at[k, step], z_peer(at, step))

    def block(self, k, step, second, x, y):
        at = self.at
        ref = self.bufs[k].at[x, at["c"], self.source(step), y]
        src = self.own[k] if isinstance(step, int) and step == 0 else ref
        if second:
            return remote(src, ref, self.ssend.at[k, step], self.srecv.at[k, step], at["second"])
        return remote(src, ref, self.fsend.at[k, step], self.frecv.at[k, step], at["first"])

    def line(self, k, kind, x, c, y):
        at = self.at
        ref = self.bufs[k].at[x, c, :, y]
        peer = at["second"] if kind == 0 else at["sibling"]
        return remote(ref, ref, self.psend.at[k, kind], self.precv.at[k, kind], peer)

    def places(self):
        at = self.at
        x, y = at["x"], at["y"]
        return (x, y), (at["fx"], at["fy"]), (at["sx"], at["sy"]), (1 - x, 1 - y)

    def start_own(self, k):
        me = self.places()[0]
        self.block(k, 0, False, *me).start()
        self.block(k, 0, True, *me).start()

    def start_z(self, k):
        self.place(k).start()

        @pl.loop(1, self.at["zs"])
        def _(step):
            self.along_z(k, step, self.at["z"]).start()

    def after_z(self, k):
        me = self.places()[0]

        @pl.loop(1, self.at["zs"])
        def _(step):
            self.along_z(k, step, self.source(step)).wait_recv()
            self.block(k, step, False, *me).start()
            self.block(k, step, True, *me).start()

        self.place(k).wait()
        self.line(k, 1, me[0], self.at["c"], me[1]).start()

    def after_first(self, k):
        first = self.places()[1]
        self.block(k, 0, False, *first).wait_recv()

        @pl.loop(1, self.at["zs"])
        def _(step):
            self.block(k, step, False, *first).wait_recv()

        self.line(k, 0, first[0], self.at["c"], first[1]).start()
        self.line(k, 2, first[0], self.at["c"], first[1]).start()

    def after_second(self, k):
        _, _, second, across = self.places()
        c = self.at["c"]
        self.block(k, 0, True, *second).wait_recv()

        @pl.loop(1, self.at["zs"])
        def _(step):
            self.block(k, step, True, *second).wait_recv()

        self.line(k, 3, second[0], c, second[1]).start()
        self.line(k, 0, across[0], c, across[1]).wait_recv()
        self.line(k, 4, across[0], c, across[1]).start()

    def done(self, k):
        me, first, second, across = self.places()
        c = 1 - self.at["c"]
        for kind, (x, y) in ((1, me), (2, second), (3, first), (4, across)):
            self.line(k, kind, x, c, y).wait_recv()

    def drain(self, k):
        me, first, second, across = self.places()
        c = self.at["c"]
        self.block(k, 0, False, *me).wait_send()
        self.block(k, 0, True, *me).wait_send()

        @pl.loop(1, self.at["zs"])
        def _(step):
            self.along_z(k, step, self.at["z"]).wait_send()
            self.block(k, step, False, *me).wait_send()
            self.block(k, step, True, *me).wait_send()

        self.line(k, 0, first[0], c, first[1]).wait_send()
        for kind, (x, y) in ((1, me), (2, first), (3, second), (4, across)):
            self.line(k, kind, x, c, y).wait_send()


def dg(left, right, dims):
    return lax.dot_general(left, right, dims, preferred_element_type=F32)


NN = (((1,), (0,)), ((), ()))
NT = (((1,), (1,)), ((), ()))
TN = (((0,), (0,)), ((), ()))
CHUNK = 64


def by_rows(rows, body):
    whole = rows // CHUNK

    @pl.loop(0, whole)
    def _(i):
        body(pl.ds(pl.multiple_of(i * CHUNK, CHUNK), CHUNK))

    if rows % CHUNK:
        body(pl.ds(whole * CHUNK, rows % CHUNK))


def norm_parts(values):
    centre = values - jnp.mean(values, axis=-1, keepdims=True)
    inverse = lax.rsqrt(jnp.mean(centre * centre, axis=-1, keepdims=True) + EPS)
    return centre * inverse, inverse


def attend_pair(p, q, k, v, mixed, log):
    cols = pl.ds(pl.multiple_of(p * 2 * HD, 2 * HD), 2 * HD)
    lane = lax.broadcasted_iota(jnp.int32, (1, 2 * HD), 1)
    scale = BF(1.0 / math.sqrt(HD))
    qp, kp, vp = q[:, cols], k[:, cols], v[:, cols]
    outs = []
    for h in range(2):
        qm = jnp.where(lane // HD == h, qp * scale, BF(0))
        scores = dg(kp, qm, NT)
        highest = jnp.max(scores, axis=0, keepdims=True)
        expo = jnp.exp(scores - highest)
        total = jnp.sum(expo, axis=0, keepdims=True)
        probs = (expo * (1.0 / total)).astype(BF)
        outs.append(dg(probs, vp, TN))
        log[p, h : h + 1, :] = highest + jnp.log(total)
    mixed[:, cols] = jnp.where(lane < HD, outs[0], outs[1]).astype(BF)


N_OWN = 7
PUMPS = {
    "LN1": 2,
    "qk": (1, 0, 0, 3),
    "v": (0, 0, 1, 0),
    "att": (0, 1, 1, 0, 0, 2, 0, 1),
    "out": 1,
    "LN2": 0,
    "up": (0, 0, 2, 0, 1, 0, 1, 0),
    "dd": (1, 0, 1, 0),
    "dn": (0, 1, 0, 2, 0, 0, 0, 0),
    "up_grad": (1, 0),
    "up_back": (0, 0, 2, 1),
    "LN2_back": 0,
    "att_back": (0, 3, 1, 0, 0, 2, 1, 1),
    "vo_grad": 3,
    "qk_grad": 1,
    "qkv_back": (0, 4, 1, 1),
}


def place_vectors(at, biases, vectors, own, pad, long, slab):
    query_bias, value_bias, up_bias = biases
    dp = at["dp"]
    heads, w = query_bias.shape
    pad[...] = jnp.zeros_like(pad)
    sums = jnp.zeros(pad.shape, F32)
    for h in range(heads):
        pad[0:1, :w] = query_bias[h : h + 1, :]
        pad[1:2, :w] = value_bias[h : h + 1, :]
        sums += pltpu.roll(pad[...], h * HD + dp * w, 1)
    pad[...] = jnp.zeros_like(pad)
    w = up_bias.shape[1]
    for odd in range(2):
        for i in range(4):
            pad[2 + i : 3 + i, :w] = up_bias[2 * i + odd : 2 * i + odd + 1, :]
        sums += pltpu.roll(pad[...], 128 * odd + dp * w, 1)
    slab[0:8, :] = sums
    slab[8:16, :] = jnp.zeros((8, 256), F32)
    long[...] = jnp.zeros_like(long)
    for i, vector in enumerate(vectors):
        long[i : i + 1, : vector.shape[1]] = vector[...]
    long[...] = pltpu.roll(long[...], dp * vectors[0].shape[1], 1)
    for pair in range(2):
        for i in range(4):
            row = 6 + 4 * pair + i
            slab[row : row + 1, :] = long[pl.ds(2 * at["tn"] + pair, 1), i * 256 : (i + 1) * 256]
    own[...] = slab[...].astype(BF)


def forward_kernel(zs, tokens, cot, mask, *refs):
    n = N_OWN
    biases, vectors, (wq, wk, wv, wo, wu, wd), refs = refs[:3], refs[3:9], refs[9:15], refs[15:]
    (block_out, w1, w2, w3, w4, w5, w6, attn_in, q, k, v, mixed, log, middle, mlp_in, factor, grad_out, pd0, pd1, dvec) = refs[:20]
    own0, own1, own2, own3, own4, own5, own6, vbuf, vecs, slots, acc, hidden, stage, pad, long, slab, slot_sem, stage_sem = refs[20:38]
    sems = refs[38:]
    own = [own0, own1, own2, own3, own4, own5, own6]
    bufs = [vbuf, w1, w2, w3, w4, w5, w6]
    rows, dim = tokens.shape
    hw = wq.shape[1]
    half = wu.shape[1] // 2
    at = coords(zs)
    g = Gather(at, own, bufs, sems)

    place_vectors(at, biases, vectors, own[0], pad, long, slab)
    own[1][:, :hw] = wq[...].astype(BF)
    own[1][:, hw:] = wk[...].astype(BF)
    enter(at)
    for i in (0, 1):
        g.start_z(i)
        g.start_own(i)
    own[2][:, :hw] = wv[...].astype(BF)
    own[2][:, hw:] = wo[...].T.astype(BF)
    g.start_z(2)
    g.start_own(2)
    own[3][...] = wu[:, :half].astype(BF)
    own[4][...] = wu[:, half:].astype(BF)
    g.start_own(3)
    g.start_own(4)
    own[5][...] = wd[:half, :].T.astype(BF)
    own[6][...] = wd[half:, :].T.astype(BF)

    def after_z(i):
        g.after_z(i)
        if i + 2 < n and i > 0:
            g.start_z(i + 2)
            if i + 2 > 4:
                g.start_own(i + 2)

    steps = [(after_z, 0), (after_z, 1), (g.after_first, 0), (g.after_second, 0), (g.done, 0)]
    steps += [(g.after_first, 1), (after_z, 2), (g.after_second, 1), (g.done, 1)]
    for i in range(2, n):
        steps += [(g.after_first, i)]
        if i + 1 < n:
            steps += [(after_z, i + 1)]
        steps += [(g.after_second, i), (g.done, i)]
    steps = list(reversed(steps))

    def until(what, i):
        while (what, i) in steps:
            step = steps.pop()
            step[0](step[1])

    def pump(count=1):
        for _ in range(count):
            if steps:
                step = steps.pop()
                step[0](step[1])

    def tile_copy(i, t):
        src = bufs[i].at[t // 2, t % 2]
        return pltpu.make_async_copy(src, slots.at[i % 2, t], slot_sem.at[t])

    def tile(i, t):
        tile_copy(i, t).wait()
        return slots[i % 2, t].reshape(dim, -1)

    def fetch(i):
        until(g.done, i)
        for t in range(4):
            tile_copy(i, t).start()

    def tiles(i, pumps, body):
        fetch(i)
        spans(pumps, pump, lambda t: body(t, tile(i, t)))

    until(g.done, 0)
    for t in range(4):
        vecs[t] = jnp.sum(vbuf[t // 2, t % 2].astype(F32).reshape(-1, *vbuf.shape[4:]), axis=0)
    for t in range(3):
        for pair in range(2):
            first = 6 + 4 * pair
            dvec[2 * t + pair : 2 * t + pair + 1, :] = jnp.concatenate(
                [vecs[t, first + i : first + i + 1, :] for i in range(4)], axis=1
            )

    keep = mask[at["tn"]].astype(F32)

    def norm_a(sl):
        grad_out[sl, :] = (cot[sl, :].astype(F32) * keep).astype(BF)
        normed, _ = norm_parts(tokens[sl, :].astype(F32))
        attn_in[sl, :] = (normed * dvec[0:1, :] + dvec[1:2, :]).astype(BF)

    by_rows(rows, norm_a)
    pump(PUMPS["LN1"])

    def qk(t, w):
        both = dg(attn_in[...], w, NN)
        cols = pl.ds(pl.multiple_of(t * hw, hw), hw)
        q[:, cols] = (both[:, :hw] + vecs[t, 0:1, :]).astype(BF)
        k[:, cols] = both[:, hw:].astype(BF)

    tiles(1, PUMPS["qk"], qk)

    def vo(t, w):
        cols = pl.ds(pl.multiple_of(t * hw, hw), hw)
        v[:, cols] = (dg(attn_in[...], w[:, :hw], NN) + vecs[t, 1:2, :]).astype(BF)

    tiles(2, PUMPS["v"], vo)
    spans(PUMPS["att"], pump, lambda p: attend_pair(p, q, k, v, mixed, log))
    acc[...] = jnp.zeros_like(acc)

    @pl.loop(0, 4)
    def _(t):
        cols = pl.ds(pl.multiple_of(t * hw, hw), hw)
        w = slots[0, t].reshape(dim, -1)[:, hw:]
        acc[...] += dg(mixed[:, cols], w, NT)

    pump(PUMPS["out"])

    def norm_m(sl):
        mid = tokens[sl, :].astype(F32) + acc[sl, :] + dvec[4:5, :]
        middle[sl, :] = mid
        normed, _ = norm_parts(mid)
        mlp_in[sl, :] = (normed * dvec[2:3, :] + dvec[3:4, :]).astype(BF)

    by_rows(rows, norm_m)
    pump(PUMPS["LN2"])

    def up(which):
        def body(t, w):
            bias = jnp.concatenate(
                [vecs[t, 2 + 2 * which + i : 3 + 2 * which + i, :] for i in range(2)], axis=1
            )
            pre = dg(mlp_in[...], w, NN) + bias
            sigma = 0.5 + 0.5 * jnp.tanh((0.5 * SLOPE) * pre)
            hid = pre * sigma
            hidden[which * 4 + t] = hid.astype(BF)
            factor[which * 4 + t] = (sigma + SLOPE * hid * (1.0 - sigma)).astype(BF)

        return body

    tiles(3, PUMPS["up"][:4], up(0))
    tiles(4, PUMPS["up"][4:], up(1))
    acc[...] = jnp.zeros_like(acc)

    def stage_copy(part, t, slot):
        return pltpu.make_async_copy(stage.at[slot], part.at[t // 2, t % 2], stage_sem.at[slot])

    def down_terms(t):
        for slot, part in enumerate((pd0, pd1)):
            terms = dg(grad_out[...], hidden[slot * 4 + t], TN).astype(BF)

            @pl.when(t > 0)
            def _():
                stage_copy(part, t - 1, slot).wait()

            stage[slot] = terms.reshape(stage.shape[1:])
            stage_copy(part, t, slot).start()

    spans(PUMPS["dd"], pump, down_terms)

    def down(which):
        def body(t, w):
            j = which * 4 + t
            acc[...] += dg(hidden[j], w, NT)
            grad_hidden = dg(grad_out[...], w, NN)
            factor[j] = (grad_hidden * factor[j].astype(F32)).astype(BF)

        return body

    tiles(5, PUMPS["dn"][:4], down(0))
    tiles(6, PUMPS["dn"][4:], down(1))

    def finish(sl):
        block_out[sl, :] = ((middle[sl, :] + acc[sl, :] + dvec[5:6, :]) * keep).astype(BF)

    by_rows(rows, finish)
    pump(len(steps))
    for slot, part in enumerate((pd0, pd1)):
        stage_copy(part, 3, slot).wait()
    for i in range(n):
        g.drain(i)


def forward(tokens, cot, mask, biases, vectors, weights, zs):
    rows, dim = tokens.shape
    wq, wk, wv, wo, wu, wd = weights
    r, hw = wq.shape
    half = wu.shape[1] // 2
    width = 2 * hw
    n = N_OWN
    vmem, hbm = pl.BlockSpec(memory_space=pltpu.VMEM), pl.BlockSpec(memory_space=pl.ANY)
    act = jax.ShapeDtypeStruct((rows, dim), BF)
    big = jax.ShapeDtypeStruct((8, rows, half), BF)
    heads = dim // HD
    outs = (
        [act]
        + [jax.ShapeDtypeStruct((2, 2, zs, 2, r, w), BF) for w in (width, width, half, half, half, half)]
        + [act] * 5
        + [jax.ShapeDtypeStruct((heads // 2, 2, rows), F32), jax.ShapeDtypeStruct((rows, dim), F32), act, big, act]
        + [jax.ShapeDtypeStruct((2, 2, zs, 2, r, half), BF)] * 2
        + [jax.ShapeDtypeStruct((8, dim), F32)]
    )
    return pl.pallas_call(
        functools.partial(forward_kernel, zs),
        out_shape=outs,
        in_specs=[vmem, vmem, pl.BlockSpec(memory_space=pltpu.SMEM)] + [vmem] * 15,
        out_specs=[vmem] + [hbm] * 6 + [vmem] * 10 + [hbm] * 2 + [vmem],
        scratch_shapes=[pltpu.VMEM((16, 256), BF)]
        + [pltpu.VMEM((r, w), BF) for w in (width, width, half, half, half, half)]
        + [
            pltpu.VMEM((2, 2, zs, 2, 16, 256), BF),
            pltpu.VMEM((4, 16, 256), F32),
            pltpu.VMEM((2, 4, zs, 2, r, half), BF),
            pltpu.VMEM((rows, dim), F32),
            pltpu.VMEM((8, rows, half), BF),
            pltpu.VMEM((2, zs, 2, r, half), BF),
            pltpu.VMEM((8, 256), F32),
            pltpu.VMEM((8, dim), F32),
            pltpu.VMEM((16, 256), F32),
            pltpu.SemaphoreType.DMA((4,)),
            pltpu.SemaphoreType.DMA((2,)),
            pltpu.SemaphoreType.DMA((n,)),
        ]
        + [pltpu.SemaphoreType.DMA((n, zs))] * 6
        + [pltpu.SemaphoreType.DMA((n, 5))] * 2,
        compiler_params=pltpu.CompilerParams(
            collective_id=0, has_side_effects=True, vmem_limit_bytes=58 * 1024 * 1024
        ),
        name="forward",
    )(tokens, cot, mask, *biases, *vectors, *weights)


class Scatter:
    def __init__(self, at, kept, rs, rf, rz, stage, sems):
        self.at, self.kept, self.rs, self.rf, self.rz, self.stage = at, kept, rs, rf, rz, stage
        self.csend, self.crecv, self.psend, self.precv, self.zsend, self.zrecv, self.local = sems

    def places(self):
        at = self.at
        x, y = at["x"], at["y"]
        return (x, y), (at["fx"], at["fy"]), (at["sx"], at["sy"]), (1 - x, 1 - y)

    def to_sibling(self, k, x, src):
        return remote(src, self.kept.at[k, x], self.csend.at[k, x], self.crecv.at[k, x], self.at["sibling"])

    def to_second(self, k, which):
        x, y = self.places()[2 + which]
        src = self.kept.at[k, x, :, y]
        return remote(src, self.rs.at[k, which], self.psend.at[k, which], self.precv.at[k, which], self.at["second"])

    def to_first(self, k):
        x, y = self.places()[1]
        src = self.kept.at[k, x, :, y]
        return remote(src, self.rf.at[k], self.psend.at[k, 2], self.precv.at[k, 2], self.at["first"])

    def along_z(self, k, step):
        at = self.at
        src = self.kept.at[k, at["x"], lax.rem(at["z"] + step, at["zs"]), at["y"]]
        return remote(src, self.rz.at[k, step], self.zsend.at[k, step], self.zrecv.at[k, step], z_peer(at, step))

    def fetch(self, k, which):
        return pltpu.make_async_copy(self.rs.at[k, which], self.stage.at[which], self.local.at[which])

    def start(self, k):
        self.to_second(k, 1).start()
        self.to_second(k, 0).start()

    def add(self, k, place, ref):
        x, y = place

        @pl.loop(0, self.at["zs"])
        def _(i):
            self.kept[k, x, i, y] = (self.kept[k, x, i, y].astype(F32) + ref[i].astype(F32)).astype(BF)

    def pass_on(self, k):
        self.to_second(k, 1).wait_recv()
        self.fetch(k, 1).start()
        self.fetch(k, 1).wait()
        self.add(k, self.places()[1], self.stage.at[1])
        self.to_first(k).start()

    def after_second(self, k):
        self.to_second(k, 0).wait_recv()
        self.fetch(k, 0).start()
        self.fetch(k, 0).wait()
        self.add(k, self.places()[0], self.stage.at[0])

    def after_first(self, k):
        self.to_first(k).wait_recv()
        self.add(k, self.places()[0], self.rf.at[k])

        @pl.loop(1, self.at["zs"])
        def _(step):
            self.along_z(k, step).start()

    def total(self, k):
        at = self.at

        @pl.loop(1, at["zs"])
        def _(step):
            self.along_z(k, step).wait_recv()

        out = self.kept[k, at["x"], at["z"], at["y"]].astype(F32)
        return lax.fori_loop(1, at["zs"], lambda step, sums: sums + self.rz[k, step].astype(F32), out)

    def drain(self, k):
        self.to_second(k, 0).wait_send()
        self.to_second(k, 1).wait_send()
        self.to_first(k).wait_send()

        @pl.loop(1, self.at["zs"])
        def _(step):
            self.along_z(k, step).wait_send()


def spans(pumps, pump, body):
    def run(first, last):
        @pl.loop(first, last)
        def _(i):
            body(i)

    start = 0
    for i, count in enumerate(pumps):
        if count or i == len(pumps) - 1:
            run(start, i + 1)
            pump(count)
            start = i + 1


def attend_pair_back(p, q, k, v, grad, log):
    cols = pl.ds(pl.multiple_of(p * 2 * HD, 2 * HD), 2 * HD)
    lane = lax.broadcasted_iota(jnp.int32, (1, 2 * HD), 1)
    scale = BF(1.0 / math.sqrt(HD))
    qp, kp, vp, gp = q[:, cols], k[:, cols], v[:, cols], grad[:, cols]
    gq = gk = gv = 0.0
    for h in range(2):
        on = lane // HD == h
        qm = jnp.where(on, qp * scale, BF(0))
        km = jnp.where(on, kp * scale, BF(0))
        gm = jnp.where(on, gp, BF(0))
        probs = jnp.exp(dg(kp, qm, NT) - log[p, h : h + 1, :])
        gv += dg(probs.astype(BF), gm, NN)
        grad_probs = dg(vp, gm, NT)
        inner = jnp.sum(probs * grad_probs, axis=0, keepdims=True)
        grad_scores = (probs * (grad_probs - inner)).astype(BF)
        gk += dg(grad_scores, qm, NN)
        gq += dg(grad_scores, km, TN)
    q[:, cols] = gq.astype(BF)
    k[:, cols] = gk.astype(BF)
    v[:, cols] = gv.astype(BF)


N_PART = 6


def backward_kernel(zs, *refs):
    n = N_PART
    pd0, pd1, w1, w2, w3, w4 = refs[:6]
    loads, dvec = refs[6:17], refs[17]
    tokens_grad, gq_out, gk_out, gv_out, go_out, gu_out, gd_out, small_out, rs = refs[18:27]
    held = refs[27:37]
    (kept, send, rf, rz, stage, wt, acc, grad_mixed, grad_attn, dsum, small, small_in, load_sem, wt_sem) = refs[37:51]
    sems = refs[51:58]
    vsend, vrecv = refs[58:]
    mlp_in, grad_pre, grad_out, middle, mixed, q, k, v, log, attn_in = held
    tokens = grad_mixed
    held = held + (tokens,)
    rows, dim = tokens.shape
    hw = gq_out.shape[1]
    at = coords(zs)
    c = at["c"]
    s = Scatter(at, kept, rs, rf, rz, stage, sems)
    names = {id(ref): i for i, ref in enumerate(held)}

    def load(ref):
        i = names[id(ref)]
        return pltpu.make_async_copy(loads[i], ref, load_sem.at[i])

    for ref in held[:-1]:
        load(ref).start()
    enter(at)

    for i, part in enumerate((pd0, pd1)):
        for x in range(2):
            s.to_sibling(i, x, part.at[x, 1 - c]).start()

    def tile_copy(src, t, slot):
        return pltpu.make_async_copy(src.at[t // 2, t % 2], wt.at[slot], wt_sem.at[slot])

    for i, part in enumerate((pd0, pd1)):
        for x in range(2):
            tile_copy(part, 2 * x + c, x).start()
        for x in range(2):
            tile_copy(part, 2 * x + c, x).wait()
            s.to_sibling(i, x, part.at[x, 1 - c]).wait_recv()

            @pl.loop(0, 2 * zs)
            def _(b):
                own = wt[x, b // 2, b % 2].astype(F32)
                kept[i, x, b // 2, b % 2] = (kept[i, x, b // 2, b % 2].astype(F32) + own).astype(BF)

        s.start(i)

    def finish(i):
        sums = s.total(i)
        half = sums.shape[1]
        if i < 2:
            gd_out[i * half : (i + 1) * half, :] = sums.T
        elif i < 4:
            gu_out[:, (i - 2) * half : (i - 1) * half] = sums
        elif i == 4:
            gv_out[...] = sums[:, :hw]
            go_out[...] = sums[:, hw:].T
        else:
            gq_out[...] = sums[:, :hw]
            gk_out[...] = sums[:, hw:]

    steps = []
    for i in range(n + 1):
        if i < n:
            steps += [(s.pass_on, i), (s.after_second, i), (s.after_first, i)]
        if i > 0:
            steps += [(finish, i - 1)]
    steps = list(reversed(steps))

    def pump(count=1):
        for _ in range(count):
            if steps:
                step = steps.pop()
                step[0](step[1])

    def produce(i, product):
        slot = i % 2
        if i - 2 >= 2:
            for x in range(2):
                s.to_sibling(i - 2, x, send.at[slot, x]).wait_send()

        @pl.loop(0, 2)
        def _(x):
            send[slot, x] = product(2 * x + 1 - c).astype(BF).reshape(send.shape[2:])
            s.to_sibling(i, x, send.at[slot, x]).start()

        @pl.loop(0, 2)
        def _(x):
            own = product(2 * x + c)
            s.to_sibling(i, x, send.at[slot, x]).wait_recv()
            other = kept[i, x].reshape(dim, -1).astype(F32)
            kept[i, x] = (own + other).astype(BF).reshape(send.shape[2:])

        s.start(i)

    def columns(t):
        return pl.ds(pl.multiple_of(t * hw, hw), hw)

    load(mlp_in).wait()
    load(grad_pre).wait()
    for which in range(2):
        produce(2 + which, lambda t: dg(mlp_in[...], grad_pre[which * 4 + t], TN))
        pump(PUMPS["up_grad"][which])

    for slot, w in enumerate((w3, w4)):
        tile_copy(w, 0, slot).start()
    acc[...] = jnp.zeros_like(acc)

    def up_back(t):
        for slot, w in enumerate((w3, w4)):
            tile_copy(w, t, slot).wait()
            acc[...] += dg(grad_pre[slot * 4 + t], wt[slot].reshape(dim, -1), NT)

            @pl.when(t < 3)
            def _():
                tile_copy(w, t + 1, slot).start()

    spans(PUMPS["up_back"], pump, up_back)
    for t in range(2):
        tile_copy(w2, t, t).start()
    for t in range(4):
        for which in range(2):
            sums = jnp.sum(grad_pre[which * 4 + t].astype(F32), axis=0, keepdims=True)
            for i in range(2):
                row = 2 + 2 * which + i
                small[t, row : row + 1, :] = sums[:, i * 256 : (i + 1) * 256]

    dsum[...] = jnp.zeros_like(dsum)
    load(middle).wait()
    load(grad_out).wait()

    def norm_back(values, grad, gain, sl, at_row):
        normed, inverse = norm_parts(values)
        scaled = grad * gain
        dsum[at_row : at_row + 1, :] += jnp.sum(grad * normed, axis=0, keepdims=True)
        dsum[at_row + 1 : at_row + 2, :] += jnp.sum(grad, axis=0, keepdims=True)
        return inverse * (
            scaled
            - jnp.mean(scaled, axis=-1, keepdims=True)
            - normed * jnp.mean(scaled * normed, axis=-1, keepdims=True)
        )

    def norm_m(sl):
        through = grad_out[sl, :].astype(F32)
        grad = through + norm_back(middle[sl, :], acc[sl, :], dvec[2:3, :], sl, 2)
        dsum[4:5, :] += jnp.sum(grad, axis=0, keepdims=True)
        dsum[5:6, :] += jnp.sum(through, axis=0, keepdims=True)
        tokens_grad[sl, :] = grad
        grad_attn[sl, :] = grad.astype(BF)

    by_rows(rows, norm_m)
    pump(PUMPS["LN2_back"])

    @pl.loop(0, 4)
    def _(t):
        slot = lax.rem(t, 2)
        tile_copy(w2, t, slot).wait()
        grad_mixed[:, columns(t)] = dg(grad_attn[...], wt[slot].reshape(dim, -1)[:, hw:], NN).astype(BF)

        @pl.when(t < 2)
        def _():
            tile_copy(w2, t + 2, slot).start()

    for ref in (q, k, v, log, mixed, attn_in):
        load(ref).wait()
    spans(PUMPS["att_back"], pump, lambda p: attend_pair_back(p, q, k, v, grad_mixed, log))
    load(tokens).start()

    def vo(t):
        return jnp.concatenate(
            [dg(attn_in[...], v[:, columns(t)], TN), dg(grad_attn[...], mixed[:, columns(t)], TN)], axis=1
        )

    def qk(t):
        return jnp.concatenate(
            [dg(attn_in[...], q[:, columns(t)], TN), dg(attn_in[...], k[:, columns(t)], TN)], axis=1
        )

    for slot, w in enumerate((w1, w2)):
        tile_copy(w, 0, slot).start()
    produce(4, vo)
    pump(PUMPS["vo_grad"])
    produce(5, qk)
    pump(PUMPS["qk_grad"])
    for t in range(4):
        cols = slice(t * hw, (t + 1) * hw)
        small[t, 0:1, :] = jnp.sum(q[:, cols].astype(F32), axis=0, keepdims=True)
        small[t, 1:2, :] = jnp.sum(v[:, cols].astype(F32), axis=0, keepdims=True)
    acc[...] = jnp.zeros_like(acc)

    def qkv_back(t):
        cols = columns(t)
        tile_copy(w1, t, 0).wait()
        both = jnp.concatenate([q[:, cols], k[:, cols]], axis=1)
        acc[...] += dg(both, wt[0].reshape(dim, -1), NT)
        tile_copy(w2, t, 1).wait()
        acc[...] += dg(v[:, cols], wt[1].reshape(dim, -1)[:, :hw], NT)

        @pl.when(t < 3)
        def _():
            tile_copy(w1, t + 1, 0).start()
            tile_copy(w2, t + 1, 1).start()

    spans(PUMPS["qkv_back"], pump, qkv_back)
    load(tokens).wait()

    def norm_a(sl):
        values = tokens[sl, :].astype(F32)
        tokens_grad[sl, :] += norm_back(values, acc[sl, :], dvec[0:1, :], sl, 0)

    by_rows(rows, norm_a)
    for t in range(4):
        small[t, 6:16, :] = jnp.zeros((10, 256), F32)
    for i in range(6):
        for j in range(4):
            row = 6 + 4 * (i % 2) + j
            small[i // 2, row : row + 1, :] = dsum[i : i + 1, j * 256 : (j + 1) * 256]
    x, y = at["x"], at["y"]
    peers = [at["sibling"], (at["dp"], at["tn"] + 2 - 4 * x), (at["dp"] + 1 - 2 * y, at["tn"])]

    def swap(i):
        return remote(small, small_in.at[i], vsend.at[i], vrecv.at[i], peers[i])

    def swap_z(step):
        return remote(small, small_in.at[2 + step], vsend.at[2 + step], vrecv.at[2 + step], z_peer(at, step))

    for i in range(3):
        swap(i).start()
        swap(i).wait()
        small[...] += small_in[i]

    @pl.loop(1, zs)
    def _(step):
        swap_z(step).start()

    pump(len(steps))

    @pl.loop(1, zs)
    def _(step):
        swap_z(step).wait()

    small_out[...] = lax.fori_loop(1, zs, lambda step, sums: sums + small_in[2 + step], small[...])
    for i in range(n):
        if i < 2:
            sources = [(pd0, pd1)[i].at[x_, 1 - c] for x_ in range(2)]
        elif i >= 4:
            sources = [send.at[i % 2, x_] for x_ in range(2)]
        else:
            sources = None
        if sources is not None:
            for x_ in range(2):
                s.to_sibling(i, x_, sources[x_]).wait_send()
        s.drain(i)


def backward(parts, weights, acts, dvec, zs):
    rows, dim = acts[-1].shape
    r, width = weights[0].shape[4:]
    hw = width // 2
    n = N_PART
    vmem, hbm = pl.BlockSpec(memory_space=pltpu.VMEM), pl.BlockSpec(memory_space=pl.ANY)
    shape = jax.ShapeDtypeStruct
    outs = [
        shape((rows, dim), F32),
        shape((r, hw), F32),
        shape((r, hw), F32),
        shape((r, hw), F32),
        shape((hw, r), F32),
        shape((r, 2 * width), F32),
        shape((2 * width, r), F32),
        shape((4, 16, 256), F32),
        shape((n, 2, zs, r, width), BF),
    ]
    sem = pltpu.SemaphoreType.DMA
    return pl.pallas_call(
        functools.partial(backward_kernel, zs),
        out_shape=outs,
        in_specs=[hbm] * (len(parts) + len(weights) + len(acts)) + [vmem],
        out_specs=[vmem] * 8 + [hbm],
        scratch_shapes=[pltpu.VMEM(a.shape, a.dtype) for a in acts[:-1]]
        + [
            pltpu.VMEM((n, 2, zs, 2, r, width), BF),
            pltpu.VMEM((2, 2, zs, 2, r, width), BF),
            pltpu.VMEM((n, zs, r, width), BF),
            pltpu.VMEM((n, zs, r, width), BF),
            pltpu.VMEM((2, zs, r, width), BF),
            pltpu.VMEM((2, zs, 2, r, width), BF),
            pltpu.VMEM((rows, dim), F32),
            pltpu.VMEM((rows, dim), BF),
            pltpu.VMEM((rows, dim), BF),
            pltpu.VMEM((8, dim), F32),
            pltpu.VMEM((4, 16, 256), F32),
            pltpu.VMEM((2 + zs, 4, 16, 256), F32),
            sem((len(acts),)),
            sem((2,)),
            sem((n, 2)),
            sem((n, 2)),
            sem((n, 3)),
            sem((n, 3)),
            sem((n, zs)),
            sem((n, zs)),
            sem((2,)),
            sem((2 + zs,)),
            sem((2 + zs,)),
        ],
        compiler_params=pltpu.CompilerParams(
            collective_id=1, has_side_effects=True, vmem_limit_bytes=60 * 1024 * 1024
        ),
        name="backward",
    )(*parts, *weights, *acts, dvec)[:8]


def finish_kernel(n, *refs):
    big, sums, big_out, refs = refs[:n], refs[n], refs[n + 1 : 2 * n + 1], refs[2 * n + 1 :]
    biases, vectors, held, (in_sem, out_sem) = refs[:3], refs[3:9], refs[9 : 9 + n], refs[9 + n :]
    reads = [pltpu.make_async_copy(big[i], held[i], in_sem.at[i]) for i in range(n)]
    copies = [pltpu.make_async_copy(held[i], big_out[i], out_sem.at[i]) for i in range(n)]
    for read in reads:
        read.start()
    for read, copy in zip(reads, copies):
        read.wait()
        copy.start()
    dp, tn = lax.axis_index("dp"), lax.axis_index("tensor")
    here = sums[tn]

    def at_lane(rows, lane):
        return pltpu.roll(rows, lax.rem(256 - lane, 256), 1)

    heads, w = biases[0].shape
    for h in range(heads):
        moved = at_lane(here, h * HD + dp * w)
        biases[0][h : h + 1, :] = moved[0:1, :w]
        biases[1][h : h + 1, :] = moved[1:2, :w]
    w = biases[2].shape[1]
    for odd in range(2):
        moved = at_lane(here, 128 * odd + dp * w)
        for i in range(4):
            biases[2][2 * i + odd : 2 * i + odd + 1, :] = moved[2 + i : 3 + i, :w]
    for i in range(6):
        w = vectors[i].shape[1]
        slab = sums[i // 2]
        lane = dp * w
        first = 6 + 4 * (i % 2)
        moved = at_lane(slab, lane % 256)
        rows = lax.broadcasted_iota(jnp.int32, moved.shape, 0)
        row = jnp.sum(jnp.where(rows == first + lane // 256, moved, 0.0), axis=0, keepdims=True)
        vectors[i][...] = row[:, :w]
    for copy in copies:
        copy.wait()


def finish(big, sums, like):
    n = len(big)
    vmem, hbm = pl.BlockSpec(memory_space=pltpu.VMEM), pl.BlockSpec(memory_space=pl.ANY)
    return pl.pallas_call(
        functools.partial(finish_kernel, n),
        out_shape=[jax.ShapeDtypeStruct(a.shape, a.dtype) for a in (*big, *like)],
        in_specs=[hbm] * n + [vmem],
        out_specs=[hbm] * n + [vmem] * len(like),
        scratch_shapes=[pltpu.VMEM(a.shape, a.dtype) for a in big] + [pltpu.SemaphoreType.DMA((n,))] * 2,
        name="finish",
    )(*big, sums)


def on_device(
    tokens,
    cotangent,
    image_mask,
    query_weight,
    key_weight,
    value_weight,
    out_weight,
    up_weight,
    down_weight,
    query_bias,
    value_bias,
    up_bias,
    attn_gain,
    attn_shift,
    mlp_gain,
    mlp_shift,
    out_bias,
    down_bias,
):
    zs = lax.axis_size("dp") // 2
    biases = (query_bias, value_bias, up_bias)
    vectors = tuple(v.reshape(1, -1) for v in (attn_gain, attn_shift, mlp_gain, mlp_shift, out_bias, down_bias))
    weights = (query_weight, key_weight, value_weight, out_weight, up_weight, down_weight)
    (block_out, w1, w2, w3, w4, _, _, attn_in, query, key, value, mixed, log, middle, mlp_in, grad_pre, grad_out, pd0, pd1, dvec) = forward(
        tokens, cotangent, image_mask, biases, vectors, weights, zs
    )
    acts = (mlp_in, grad_pre, grad_out, middle, mixed, query, key, value, log, attn_in, tokens)
    grads = backward((pd0, pd1), (w1, w2, w3, w4), acts, dvec, zs)
    done = finish((block_out, *grads[:7]), grads[7], biases + vectors)
    return tuple(done[:11]) + tuple(v.reshape(-1) for v in done[11:])


def solution(mesh):
    wide, tall = P("dp", "tensor"), P("tensor", "dp")
    rows = P(("dp", "tensor"), None)
    weights = (wide, wide, wide, tall, wide, tall, tall, tall, tall)
    vectors = (P("dp"),) * 6
    return jax.shard_map(
        on_device,
        mesh=mesh,
        in_specs=(rows, rows, P("dp")) + weights + vectors,
        out_specs=(rows, rows) + weights + vectors,
        check_vma=False,
    )
```

```python
import functools
import math

import jax
import jax.numpy as jnp
from jax import lax
from jax.experimental import pallas as pl
from jax.experimental.pallas import tpu as pltpu
from jax.sharding import PartitionSpec as P

HD = 64
EPS = 1e-05
SLOPE = 1.702
MESH = pl.DeviceIdType.MESH
BF = jnp.bfloat16
F32 = jnp.float32


def coords(zs):
    dp, tn = lax.axis_index("dp"), lax.axis_index("tensor")
    z, y = dp // 2, dp % 2
    x, c = tn // 2, tn % 2
    over_y = (dp + 1 - 2 * y, tn)
    over_x = (dp, tn + 2 - 4 * x)
    first = (dp + (1 - c) * (1 - 2 * y), tn + c * (2 - 4 * x))
    second = (dp + c * (1 - 2 * y), tn + (1 - c) * (2 - 4 * x))
    sibling = (dp, tn + 1 - 2 * c)
    del over_y, over_x
    fx, fy = x + c * (1 - 2 * x), y + (1 - c) * (1 - 2 * y)
    sx, sy = x + (1 - c) * (1 - 2 * x), y + c * (1 - 2 * y)
    return dict(
        dp=dp, tn=tn, z=z, y=y, x=x, c=c, first=first, second=second, sibling=sibling,
        fx=fx, fy=fy, sx=sx, sy=sy, zs=zs,
    )


def z_peer(at, step):
    return (lax.rem(at["z"] + step, at["zs"]) * 2 + at["y"], at["tn"])


def enter(at):
    barrier = pltpu.get_barrier_semaphore()
    peers = [at["first"], at["second"], at["sibling"]]
    for peer in peers:
        pl.semaphore_signal(barrier, inc=1, device_id=peer, device_id_type=MESH)

    @pl.loop(1, at["zs"])
    def _(step):
        pl.semaphore_signal(barrier, inc=1, device_id=z_peer(at, step), device_id_type=MESH)

    pl.semaphore_wait(barrier, len(peers) + at["zs"] - 1)


def remote(src, dst, send, recv, peer):
    return pltpu.make_async_remote_copy(
        src_ref=src, dst_ref=dst, send_sem=send, recv_sem=recv, device_id=peer, device_id_type=MESH
    )


class Gather:
    def __init__(self, at, own, bufs, sems):
        self.at, self.own, self.bufs = at, own, bufs
        (self.local, self.zsend, self.zrecv, self.fsend, self.frecv, self.ssend, self.srecv, self.psend, self.precv) = sems

    def place(self, k):
        at = self.at
        return pltpu.make_async_copy(
            self.own[k], self.bufs[k].at[at["x"], at["c"], at["z"], at["y"]], self.local.at[k]
        )

    def source(self, step):
        at = self.at
        return lax.rem(at["z"] - step + at["zs"], at["zs"])

    def along_z(self, k, step, z):
        at = self.at
        dst = self.bufs[k].at[at["x"], at["c"], z, at["y"]]
        return remote(self.own[k], dst, self.zsend.at[k, step], self.zrecv.at[k, step], z_peer(at, step))

    def block(self, k, step, second, x, y):
        at = self.at
        ref = self.bufs[k].at[x, at["c"], self.source(step), y]
        src = self.own[k] if isinstance(step, int) and step == 0 else ref
        if second:
            return remote(src, ref, self.ssend.at[k, step], self.srecv.at[k, step], at["second"])
        return remote(src, ref, self.fsend.at[k, step], self.frecv.at[k, step], at["first"])

    def line(self, k, kind, x, c, y):
        at = self.at
        ref = self.bufs[k].at[x, c, :, y]
        peer = at["second"] if kind == 0 else at["sibling"]
        return remote(ref, ref, self.psend.at[k, kind], self.precv.at[k, kind], peer)

    def places(self):
        at = self.at
        x, y = at["x"], at["y"]
        return (x, y), (at["fx"], at["fy"]), (at["sx"], at["sy"]), (1 - x, 1 - y)

    def start_own(self, k):
        me = self.places()[0]
        self.block(k, 0, False, *me).start()
        self.block(k, 0, True, *me).start()

    def start_z(self, k):
        self.place(k).start()

        @pl.loop(1, self.at["zs"])
        def _(step):
            self.along_z(k, step, self.at["z"]).start()

    def after_z(self, k):
        me = self.places()[0]

        @pl.loop(1, self.at["zs"])
        def _(step):
            self.along_z(k, step, self.source(step)).wait_recv()
            self.block(k, step, False, *me).start()
            self.block(k, step, True, *me).start()

        self.place(k).wait()
        self.line(k, 1, me[0], self.at["c"], me[1]).start()

    def after_first(self, k):
        first = self.places()[1]
        self.block(k, 0, False, *first).wait_recv()

        @pl.loop(1, self.at["zs"])
        def _(step):
            self.block(k, step, False, *first).wait_recv()

        self.line(k, 0, first[0], self.at["c"], first[1]).start()
        self.line(k, 2, first[0], self.at["c"], first[1]).start()

    def after_second(self, k):
        second = self.places()[2]
        c = self.at["c"]
        self.block(k, 0, True, *second).wait_recv()

        @pl.loop(1, self.at["zs"])
        def _(step):
            self.block(k, step, True, *second).wait_recv()

        self.line(k, 3, second[0], c, second[1]).start()

    def after_across(self, k):
        across = self.places()[3]
        c = self.at["c"]
        self.line(k, 0, across[0], c, across[1]).wait_recv()
        self.line(k, 4, across[0], c, across[1]).start()

    def done(self, k):
        me, first, second, across = self.places()
        c = 1 - self.at["c"]
        for kind, (x, y) in ((1, me), (2, second), (3, first), (4, across)):
            self.line(k, kind, x, c, y).wait_recv()

    def drain(self, k):
        me, first, second, across = self.places()
        c = self.at["c"]
        self.block(k, 0, False, *me).wait_send()
        self.block(k, 0, True, *me).wait_send()

        @pl.loop(1, self.at["zs"])
        def _(step):
            self.along_z(k, step, self.at["z"]).wait_send()
            self.block(k, step, False, *me).wait_send()
            self.block(k, step, True, *me).wait_send()

        self.line(k, 0, first[0], c, first[1]).wait_send()
        for kind, (x, y) in ((1, me), (2, first), (3, second), (4, across)):
            self.line(k, kind, x, c, y).wait_send()


def dg(left, right, dims):
    return lax.dot_general(left, right, dims, preferred_element_type=F32)


NN = (((1,), (0,)), ((), ()))
NT = (((1,), (1,)), ((), ()))
TN = (((0,), (0,)), ((), ()))
CHUNK = 64


def by_rows(rows, body):
    whole = rows // CHUNK

    @pl.loop(0, whole)
    def _(i):
        body(pl.ds(pl.multiple_of(i * CHUNK, CHUNK), CHUNK))

    if rows % CHUNK:
        body(pl.ds(whole * CHUNK, rows % CHUNK))


def norm_parts(values):
    centre = values - jnp.mean(values, axis=-1, keepdims=True)
    inverse = lax.rsqrt(jnp.mean(centre * centre, axis=-1, keepdims=True) + EPS)
    return centre * inverse, inverse


def attend_pair(p, q, k, v, mixed, log):
    cols = pl.ds(pl.multiple_of(p * 2 * HD, 2 * HD), 2 * HD)
    lane = lax.broadcasted_iota(jnp.int32, (1, 2 * HD), 1)
    scale = BF(1.0 / math.sqrt(HD))
    qp, kp, vp = q[:, cols], k[:, cols], v[:, cols]
    outs = []
    for h in range(2):
        qm = jnp.where(lane // HD == h, qp * scale, BF(0))
        scores = dg(kp, qm, NT)
        highest = jnp.max(scores, axis=0, keepdims=True)
        expo = jnp.exp(scores - highest)
        total = jnp.sum(expo, axis=0, keepdims=True)
        probs = (expo * (1.0 / total)).astype(BF)
        outs.append(dg(probs, vp, TN))
        log[p, h : h + 1, :] = highest + jnp.log(total)
    mixed[:, cols] = jnp.where(lane < HD, outs[0], outs[1]).astype(BF)


def place_vectors(at, biases, vectors, own, pad, long, slab):
    query_bias, value_bias, up_bias = biases
    dp = at["dp"]
    heads, w = query_bias.shape
    pad[...] = jnp.zeros_like(pad)
    sums = jnp.zeros(pad.shape, F32)
    for h in range(heads):
        pad[0:1, :w] = query_bias[h : h + 1, :]
        pad[1:2, :w] = value_bias[h : h + 1, :]
        sums += pltpu.roll(pad[...], h * HD + dp * w, 1)
    pad[...] = jnp.zeros_like(pad)
    w = up_bias.shape[1]
    for odd in range(2):
        for i in range(4):
            pad[2 + i : 3 + i, :w] = up_bias[2 * i + odd : 2 * i + odd + 1, :]
        sums += pltpu.roll(pad[...], 128 * odd + dp * w, 1)
    slab[0:8, :] = sums
    slab[8:16, :] = jnp.zeros((8, 256), F32)
    long[...] = jnp.zeros_like(long)
    for i, vector in enumerate(vectors):
        long[i : i + 1, : vector.shape[1]] = vector[...]
    long[...] = pltpu.roll(long[...], dp * vectors[0].shape[1], 1)
    for pair in range(2):
        for i in range(4):
            row = 6 + 4 * pair + i
            slab[row : row + 1, :] = long[pl.ds(2 * at["tn"] + pair, 1), i * 256 : (i + 1) * 256]
    own[...] = slab[...].astype(BF)


class Scatter:
    def __init__(self, at, kept, rs, rf, rz, stage, sems):
        self.at, self.kept, self.rs, self.rf, self.rz, self.stage = at, kept, rs, rf, rz, stage
        self.csend, self.crecv, self.psend, self.precv, self.zsend, self.zrecv, self.local = sems

    def places(self):
        at = self.at
        x, y = at["x"], at["y"]
        return (x, y), (at["fx"], at["fy"]), (at["sx"], at["sy"]), (1 - x, 1 - y)

    def to_sibling(self, k, x, src):
        return remote(src, self.kept[k].at[x], self.csend.at[k, x], self.crecv.at[k, x], self.at["sibling"])

    def to_second(self, k, which):
        x, y = self.places()[2 + which]
        src = self.kept[k].at[x, :, y]
        return remote(src, self.rs[k].at[which], self.psend.at[k, which], self.precv.at[k, which], self.at["second"])

    def to_first(self, k):
        x, y = self.places()[1]
        src = self.kept[k].at[x, :, y]
        return remote(src, self.rf[k], self.psend.at[k, 2], self.precv.at[k, 2], self.at["first"])

    def along_z(self, k, step):
        at = self.at
        src = self.kept[k].at[at["x"], lax.rem(at["z"] + step, at["zs"]), at["y"]]
        return remote(src, self.rz[k].at[step - 1], self.zsend.at[k, step], self.zrecv.at[k, step], z_peer(at, step))

    def fetch(self, k, which):
        return pltpu.make_async_copy(self.rs[k].at[which], self.staged(k, which), self.local.at[0])

    def staged(self, k, which):
        return self.stage.at[:, :, pl.ds(0, self.kept[k].shape[-1])]

    def start(self, k):
        self.to_second(k, 1).start()
        self.to_second(k, 0).start()

    def add(self, k, place, ref):
        x, y = place

        @pl.loop(0, self.at["zs"])
        def _(i):
            self.kept[k][x, i, y] += ref[i]

    def pass_on(self, k):
        self.to_second(k, 1).wait_recv()
        self.fetch(k, 1).start()
        self.fetch(k, 1).wait()
        self.add(k, self.places()[1], self.staged(k, 1))
        self.to_first(k).start()

    def after_second(self, k):
        self.to_second(k, 0).wait_recv()
        self.fetch(k, 0).start()
        self.fetch(k, 0).wait()
        self.add(k, self.places()[0], self.staged(k, 0))

    def after_first(self, k):
        self.to_first(k).wait_recv()
        self.add(k, self.places()[0], self.rf[k])

        @pl.loop(1, self.at["zs"])
        def _(step):
            self.along_z(k, step).start()

    def total(self, k):
        at = self.at

        @pl.loop(1, at["zs"])
        def _(step):
            self.along_z(k, step).wait_recv()

        width = self.kept[k].shape[-1]
        others = self.stage.at[pl.ds(0, at["zs"] - 1), :, pl.ds(0, width)]
        fetch = pltpu.make_async_copy(self.rz[k], others, self.local.at[0])
        fetch.start()
        fetch.wait()
        out = self.kept[k][at["x"], at["z"], at["y"]].astype(F32)
        return lax.fori_loop(0, at["zs"] - 1, lambda i, sums: sums + self.stage[i, :, :width].astype(F32), out)

    def drain(self, k):
        self.to_second(k, 0).wait_send()
        self.to_second(k, 1).wait_send()
        self.to_first(k).wait_send()

        @pl.loop(1, self.at["zs"])
        def _(step):
            self.along_z(k, step).wait_send()


def spans(pumps, pump, body):
    def run(first, last):
        @pl.loop(first, last)
        def _(i):
            body(i)

    start = 0
    for i, count in enumerate(pumps):
        if count or i == len(pumps) - 1:
            run(start, i + 1)
            pump(count)
            start = i + 1


def attend_pair_back(p, q, k, v, grad, log):
    cols = pl.ds(pl.multiple_of(p * 2 * HD, 2 * HD), 2 * HD)
    lane = lax.broadcasted_iota(jnp.int32, (1, 2 * HD), 1)
    scale = BF(1.0 / math.sqrt(HD))
    qp, kp, vp, gp = q[:, cols], k[:, cols], v[:, cols], grad[:, cols]
    gq = gk = gv = 0.0
    for h in range(2):
        on = lane // HD == h
        qm = jnp.where(on, qp * scale, BF(0))
        km = jnp.where(on, kp * scale, BF(0))
        gm = jnp.where(on, gp, BF(0))
        probs = jnp.exp(dg(kp, qm, NT) - log[p, h : h + 1, :])
        gv += dg(probs.astype(BF), gm, NN)
        grad_probs = dg(vp, gm, NT)
        inner = jnp.sum(probs * grad_probs, axis=0, keepdims=True)
        grad_scores = (probs * (grad_probs - inner)).astype(BF)
        gk += dg(grad_scores, qm, NN)
        gq += dg(grad_scores, km, TN)
    q[:, cols] = gq.astype(BF)
    k[:, cols] = gk.astype(BF)
    v[:, cols] = gv.astype(BF)


N_OWN = 9
N_PART = 8
ORDER = [
    ("Z", 0), ("F", 0), ("S", 0), ("Z", 1), ("T", 0), ("D", 0), ("F", 1), ("S", 1), ("Z", 2), ("Z", 3),
    ("F", 2), ("T", 1), ("Z", 4), ("D", 1), ("S", 2), ("F", 3), ("S", 3), ("F", 4), ("Z", 5), ("T", 2),
    ("D", 2), ("S", 4), ("F", 5), ("Z", 6), ("T", 3), ("D", 3), ("T", 4), ("D", 4), ("F", 6), ("Z", 7),
    ("S", 5), ("F", 7), ("T", 5), ("Z", 8), ("S", 6), ("D", 5), ("F", 8), ("T", 6), ("S", 7), ("D", 6),
    ("T", 7), ("D", 7), ("S", 8), ("T", 8), ("a", 0), ("D", 8), ("b", 0), ("e", 0), ("a", 1), ("b", 1),
    ("a", 2), ("f", 0), ("e", 1), ("b", 2), ("a", 3), ("e", 2), ("f", 1), ("b", 3), ("f", 2), ("e", 3),
    ("a", 4), ("b", 4), ("e", 4), ("f", 3), ("f", 4), ("a", 5), ("b", 5), ("a", 6), ("b", 6), ("e", 5),
    ("a", 7), ("e", 6), ("f", 5), ("b", 7), ("e", 7), ("f", 6), ("f", 7),
]
PUMPS = {
    "LN1": 3,
    "q": (0, 1, 0, 1),
    "k": (0, 1, 1, 1),
    "v": (0, 0, 0, 1),
    "att": (1, 2, 1, 0, 0, 0, 1, 2),
    "out": 2,
    "LN2": 0,
    "up": ((0, 1, 0, 1), (1, 0, 2, 0)),
    "dn": ((2, 0, 0, 1), (0, 0, 1, 0)),
    "grad": (2, 1, 2, 4, 3, 0, 0, 2),
    "up_back": ((0, 0, 0, 0), (0, 0, 0, 2)),
    "LN2_back": 1,
    "att_back": (1, 2, 0, 1, 1, 0, 0, 0),
    "qk_back": (3, 0, 0, 0),
    "v_back": (1, 0, 1, 1),
    "LN1_back": 3,
    "swap": (0, 0, 0),
}


def block_kernel(zs, tokens_in, cot, mask, *refs):
    n, parts = N_OWN, N_PART
    refs = list(refs)

    def take(count):
        got = refs[:count]
        del refs[:count]
        return got if count > 1 else got[0]

    biases, vectors = take(3), take(6)
    wq, wk, wv, wo, wu, wd = take(6)
    block_out, tokens_grad, gq_out, gk_out, gv_out, go_out, gu_out, gd_out, small_out = take(9)
    bufs, rs, rz = take(n), take(parts), take(parts)
    weights = bufs[1:]
    own = take(n)
    kept, rf = take(parts), take(parts)
    (send, stage, wt, pair, grad_out, attn_in, q, k, v, log, mixed, middle, mlp_in, hidden, grad_pre, acc) = take(16)
    vstage, vecs, dvec, dsum, pad, long, slab, small, small_in = take(9)
    load_sem, wt_sem, vsend, vrecv = take(4)
    gsems, ssems = take(9), take(7)
    tokens, grad_mixed, grad_attn = pair.at[0], pair.at[0], pair.at[1]
    rows, dim = attn_in.shape
    hw = wq.shape[1]
    half = wu.shape[1] // 2
    at = coords(zs)
    c = at["c"]
    g = Gather(at, own, bufs, gsems)
    s = Scatter(at, kept, rs, rf, rz, stage, ssems)
    w_q, w_k, w_v, w_o, w_u0, w_u1, w_d0, w_d1 = weights

    load_tokens = pltpu.make_async_copy(tokens_in, tokens, load_sem.at[0])
    load_cot = pltpu.make_async_copy(cot, grad_out, load_sem.at[1])
    load_tokens.start()
    load_cot.start()
    place_vectors(at, biases, vectors, own[0], pad, long, slab)
    own[1][...] = wq[...].astype(BF)
    own[2][...] = wk[...].astype(BF)
    enter(at)

    for i in range(3):
        g.start_z(i)
        g.start_own(i)
    own[3][...] = wv[...].astype(BF)
    own[4][...] = wo[...].T.astype(BF)
    g.start_own(3)
    g.start_own(4)
    own[5][...] = wu[:, :half].astype(BF)
    own[6][...] = wu[:, half:].astype(BF)
    own[7][...] = wd[:half, :].T.astype(BF)
    own[8][...] = wd[half:, :].T.astype(BF)

    def after_z(i):
        if i + 2 < n and i > 0:
            g.start_z(i + 2)
            if i + 2 >= 5:
                g.start_own(i + 2)
        g.after_z(i)

    def finish_part(i):
        sums = s.total(i)
        if i < 2:
            gd_out[i * half : (i + 1) * half, :] = sums.T
        elif i < 4:
            gu_out[:, (i - 2) * half : (i - 1) * half] = sums
        elif i == 4:
            go_out[...] = sums.T
        else:
            (gv_out, gq_out, gk_out)[i - 5][...] = sums

    kinds = {
        "Z": after_z, "F": g.after_first, "S": g.after_second, "T": g.after_across, "D": g.done,
        "a": s.pass_on, "b": s.after_second, "e": s.after_first, "f": finish_part,
    }
    steps = list(reversed(ORDER))

    def take_step():
        what, i = steps.pop()
        kinds[what](i)

    def pump(count=1):
        for _ in range(min(count, len(steps))):
            take_step()

    def until(what, i):
        while (what, i) in steps:
            take_step()

    def tile_copy(w, t, side=0, part=0):
        width = w.shape[-1]
        dst = wt.at[t, :, :, :, pl.ds(side * hw, width)]
        return pltpu.make_async_copy(w.at[t // 2, t % 2], dst, wt_sem.at[part, t])

    def fetch(w, side=0, part=0):
        for t in range(4):
            tile_copy(w, t, side, part).start()

    def tile(w, t, side=0, part=0):
        tile_copy(w, t, side, part).wait()
        return wt[t, :, :, :, side * hw : side * hw + w.shape[-1]].reshape(dim, -1)

    def tiles(w, pumps, body):
        spans(pumps, pump, lambda t: body(t, tile(w, t)))

    def columns(t):
        return pl.ds(pl.multiple_of(t * hw, hw), hw)

    def product(i, make):
        slot = i % 2
        width = kept[i].shape[-1]

        def out(x):
            return send.at[slot, x, :, :, :, pl.ds(0, width)]

        if i >= 2:
            for x in range(2):
                before = send.at[slot, x, :, :, :, pl.ds(0, kept[i - 2].shape[-1])]
                s.to_sibling(i - 2, x, before).wait_send()

        @pl.loop(0, 2)
        def _(x):
            send[slot, x, :, :, :, :width] = make(2 * x + 1 - c).astype(BF).reshape(kept[i].shape[1:])
            s.to_sibling(i, x, out(x)).start()

        @pl.loop(0, 2)
        def _(x):
            terms = make(2 * x + c)
            s.to_sibling(i, x, out(x)).wait_recv()
            other = kept[i][x].reshape(dim, -1).astype(F32)
            kept[i][x] = (terms + other).astype(BF).reshape(kept[i].shape[1:])

        s.start(i)
        pump(PUMPS["grad"][i])

    until("D", 0)
    for t in range(4):
        fetch_vectors = pltpu.make_async_copy(bufs[0].at[t // 2, t % 2], vstage, load_sem.at[2])
        fetch_vectors.start()
        fetch_vectors.wait()
        vecs[t] = jnp.sum(vstage[...].astype(F32).reshape(-1, 16, 256), axis=0)
    for t in range(3):
        for which in range(2):
            first = 6 + 4 * which
            dvec[2 * t + which : 2 * t + which + 1, :] = jnp.concatenate(
                [vecs[t, first + i : first + i + 1, :] for i in range(4)], axis=1
            )
    keep = mask[at["tn"]].astype(F32)
    load_tokens.wait()
    load_cot.wait()

    def norm_a(sl):
        grad_out[sl, :] = (grad_out[sl, :].astype(F32) * keep).astype(BF)
        normed, _ = norm_parts(tokens[sl, :].astype(F32))
        attn_in[sl, :] = (normed * dvec[0:1, :] + dvec[1:2, :]).astype(BF)

    by_rows(rows, norm_a)
    pump(PUMPS["LN1"])

    def project(dst, bias_row):
        def body(t, w):
            got = dg(attn_in[...], w, NN)
            if bias_row is not None:
                got = got + vecs[t, bias_row : bias_row + 1, :]
            dst[:, columns(t)] = got.astype(BF)

        return body

    for i, (w, dst, bias_row, name) in enumerate(((w_q, q, 0, "q"), (w_k, k, None, "k"), (w_v, v, 1, "v"))):
        until("D", 1 + i)
        fetch(w)
        tiles(w, PUMPS[name], project(dst, bias_row))
    spans(PUMPS["att"], pump, lambda p: attend_pair(p, q, k, v, mixed, log))
    until("D", 4)
    fetch(w_o)
    acc[...] = jnp.zeros_like(acc)

    def out_project(t, w):
        acc[...] += dg(mixed[:, columns(t)], w, NT)

    tiles(w_o, (0, 0, 0, PUMPS["out"]), out_project)

    def norm_m(sl):
        mid = tokens[sl, :].astype(F32) + acc[sl, :] + dvec[4:5, :]
        middle[sl, :] = mid
        normed, _ = norm_parts(mid)
        mlp_in[sl, :] = (normed * dvec[2:3, :] + dvec[3:4, :]).astype(BF)

    by_rows(rows, norm_m)
    pump(PUMPS["LN2"])

    def hidden_of(which, t):
        if which == 0:
            return hidden.at[t]
        return pair.at[t // 2, :, pl.ds(pl.multiple_of(t % 2 * half, half), half)]

    def up(which):
        def body(t, w):
            bias = jnp.concatenate(
                [vecs[t, 2 + 2 * which + i : 3 + 2 * which + i, :] for i in range(2)], axis=1
            )
            pre = dg(mlp_in[...], w, NN) + bias
            sigma = 0.5 + 0.5 * jnp.tanh((0.5 * SLOPE) * pre)
            hid = pre * sigma
            hidden_of(which, t)[...] = hid.astype(BF)
            grad_pre[which * 4 + t] = (sigma + SLOPE * hid * (1.0 - sigma)).astype(BF)

        return body

    for which, w in enumerate((w_u0, w_u1)):
        until("D", 5 + which)
        fetch(w)
        tiles(w, PUMPS["up"][which], up(which))
        if which == 0:
            product(0, lambda t: dg(grad_out[...], hidden_of(0, t)[...], TN))
    product(1, lambda t: dg(grad_out[...], hidden_of(1, t)[...], TN))
    acc[...] = jnp.zeros_like(acc)

    def down(which):
        def body(t, w):
            j = which * 4 + t
            acc[...] += dg(hidden_of(which, t)[...], w, NT)
            grad_hidden = dg(grad_out[...], w, NN)
            grad_pre[j] = (grad_hidden * grad_pre[j].astype(F32)).astype(BF)

        return body

    def up_terms(which):
        return lambda t: dg(mlp_in[...], grad_pre[which * 4 + t], TN)

    until("D", 7)
    fetch(w_d0)
    tiles(w_d0, PUMPS["dn"][0], down(0))
    product(2, up_terms(0))
    until("D", 8)
    fetch(w_d1)
    tiles(w_d1, PUMPS["dn"][1], down(1))
    fetch(w_u0)

    def finish_rows(sl):
        pair[0, sl, :] = ((middle[sl, :] + acc[sl, :] + dvec[5:6, :]) * keep).astype(BF)

    by_rows(rows, finish_rows)
    store_block = pltpu.make_async_copy(pair.at[0], block_out, load_sem.at[2])
    store_block.start()

    product(3, up_terms(1))
    acc[...] = jnp.zeros_like(acc)

    def up_back(which):
        def body(t, w):
            acc[...] += dg(grad_pre[which * 4 + t], w, NT)

        return body

    tiles(w_u0, PUMPS["up_back"][0], up_back(0))
    fetch(w_u1)
    tiles(w_u1, PUMPS["up_back"][1], up_back(1))
    fetch(w_o)
    dsum[...] = jnp.zeros_like(dsum)

    def norm_back(values, grad, gain, at_row):
        normed, inverse = norm_parts(values)
        scaled = grad * gain
        dsum[at_row : at_row + 1, :] += jnp.sum(grad * normed, axis=0, keepdims=True)
        dsum[at_row + 1 : at_row + 2, :] += jnp.sum(grad, axis=0, keepdims=True)
        return inverse * (
            scaled
            - jnp.mean(scaled, axis=-1, keepdims=True)
            - normed * jnp.mean(scaled * normed, axis=-1, keepdims=True)
        )

    def norm_m_back(sl):
        through = grad_out[sl, :].astype(F32)
        grad = through + norm_back(middle[sl, :], acc[sl, :], dvec[2:3, :], 2)
        dsum[4:5, :] += jnp.sum(grad, axis=0, keepdims=True)
        dsum[5:6, :] += jnp.sum(through, axis=0, keepdims=True)
        middle[sl, :] = grad
        grad_attn[sl, :] = grad.astype(BF)

    by_rows(rows, norm_m_back)
    store_block.wait()
    pump(PUMPS["LN2_back"])

    def mixed_back(t, w):
        grad_mixed[:, columns(t)] = dg(grad_attn[...], w, NN).astype(BF)

    tiles(w_o, (0, 0, 0, 0), mixed_back)
    product(4, lambda t: dg(grad_attn[...], mixed[:, columns(t)], TN))
    fetch(w_q, 0, 0)
    fetch(w_k, 1, 1)
    spans(PUMPS["att_back"], pump, lambda p: attend_pair_back(p, q, k, v, grad_mixed, log))
    reload_tokens = pltpu.make_async_copy(tokens_in, tokens, load_sem.at[0])
    reload_tokens.start()
    for i, grad in ((5, v), (6, q), (7, k)):
        product(i, lambda t, grad=grad: dg(attn_in[...], grad[:, columns(t)], TN))
    for t in range(4):
        cols = slice(t * hw, (t + 1) * hw)
        small[t, 0:1, :] = jnp.sum(q[:, cols].astype(F32), axis=0, keepdims=True)
        small[t, 1:2, :] = jnp.sum(v[:, cols].astype(F32), axis=0, keepdims=True)
        for which in range(2):
            sums = jnp.sum(grad_pre[which * 4 + t].astype(F32), axis=0, keepdims=True)
            for i in range(2):
                row = 2 + 2 * which + i
                small[t, row : row + 1, :] = sums[:, i * 256 : (i + 1) * 256]
        small[t, 6:16, :] = jnp.zeros((10, 256), F32)
    acc[...] = jnp.zeros_like(acc)

    def qk_back(t):
        tile_copy(w_q, t, 0, 0).wait()
        tile_copy(w_k, t, 1, 1).wait()
        both = jnp.concatenate([q[:, columns(t)], k[:, columns(t)]], axis=1)
        acc[...] += dg(both, wt[t].reshape(dim, -1), NT)

    spans(PUMPS["qk_back"], pump, qk_back)
    fetch(w_v)

    def v_back(t, w):
        acc[...] += dg(v[:, columns(t)], w, NT)

    tiles(w_v, PUMPS["v_back"], v_back)
    reload_tokens.wait()

    def norm_a_back(sl):
        values = tokens[sl, :].astype(F32)
        middle[sl, :] += norm_back(values, acc[sl, :], dvec[0:1, :], 0)

    by_rows(rows, norm_a_back)
    store_grad = pltpu.make_async_copy(middle, tokens_grad, load_sem.at[1])
    store_grad.start()
    pump(PUMPS["LN1_back"])
    for i in range(6):
        for j in range(4):
            row = 6 + 4 * (i % 2) + j
            small[i // 2, row : row + 1, :] = dsum[i : i + 1, j * 256 : (j + 1) * 256]
    x, y = at["x"], at["y"]
    peers = [at["sibling"], (at["dp"], at["tn"] + 2 - 4 * x), (at["dp"] + 1 - 2 * y, at["tn"])]

    def swap(i):
        return remote(small, small_in.at[i], vsend.at[i], vrecv.at[i], peers[i])

    def swap_z(step):
        return remote(small, small_in.at[2 + step], vsend.at[2 + step], vrecv.at[2 + step], z_peer(at, step))

    for i in range(3):
        swap(i).start()
        pump(PUMPS["swap"][i])
        swap(i).wait()
        small[...] += small_in[i]

    @pl.loop(1, zs)
    def _(step):
        swap_z(step).start()

    pump(len(steps))

    @pl.loop(1, zs)
    def _(step):
        swap_z(step).wait()

    small_out[...] = lax.fori_loop(1, zs, lambda step, sums: sums + small_in[2 + step], small[...])
    store_grad.wait()
    for i in range(n):
        g.drain(i)
    for i in range(parts):
        if i >= parts - 2:
            for x_ in range(2):
                out = send.at[i % 2, x_, :, :, :, pl.ds(0, kept[i].shape[-1])]
                s.to_sibling(i, x_, out).wait_send()
        s.drain(i)


def block(tokens, cot, mask, biases, vectors, weights, zs):
    rows, dim = tokens.shape
    wq, wk, wv, wo, wu, wd = weights
    r, hw = wq.shape
    half = wu.shape[1] // 2
    n, parts = N_OWN, N_PART
    vmem, hbm = pl.BlockSpec(memory_space=pltpu.VMEM), pl.BlockSpec(memory_space=pl.ANY)
    shape, sem = jax.ShapeDtypeStruct, pltpu.SemaphoreType.DMA
    own_widths = [hw] * 4 + [half] * 4
    widths = [half] * 4 + [hw] * 4
    outs = [
        shape((rows, dim), BF),
        shape((rows, dim), F32),
        shape((r, hw), F32),
        shape((r, hw), F32),
        shape((r, hw), F32),
        shape((hw, r), F32),
        shape((r, 2 * half), F32),
        shape((2 * half, r), F32),
        shape((4, 16, 256), F32),
    ]
    outs += [shape((2, 2, zs, 2, 16, 256), BF)]
    outs += [shape((2, 2, zs, 2, r, w), BF) for w in own_widths]
    outs += [shape((2, zs, r, w), BF) for w in widths]
    outs += [shape((zs - 1, r, w), BF) for w in widths]
    act, wide = pltpu.VMEM((rows, dim), BF), pltpu.VMEM((rows, dim), F32)
    return pl.pallas_call(
        functools.partial(block_kernel, zs),
        out_shape=outs,
        in_specs=[hbm, hbm, pl.BlockSpec(memory_space=pltpu.SMEM)] + [vmem] * 15,
        out_specs=[hbm] * 2 + [vmem] * 7 + [hbm] * (n + 2 * parts),
        scratch_shapes=[pltpu.VMEM((16, 256), BF)]
        + [pltpu.VMEM((r, w), BF) for w in own_widths]
        + [pltpu.VMEM((2, zs, 2, r, w), BF) for w in widths]
        + [pltpu.VMEM((zs, r, w), BF) for w in widths]
        + [
            pltpu.VMEM((2, 2, zs, 2, r, half), BF),
            pltpu.VMEM((zs, r, half), BF),
            pltpu.VMEM((4, zs, 2, r, half), BF),
            pltpu.VMEM((2, rows, dim), BF),
            act,
            act,
            act,
            act,
            act,
            pltpu.VMEM((dim // HD // 2, 2, rows), F32),
            act,
            wide,
            act,
            pltpu.VMEM((4, rows, half), BF),
            pltpu.VMEM((8, rows, half), BF),
            wide,
            pltpu.VMEM((zs, 2, 16, 256), BF),
            pltpu.VMEM((4, 16, 256), F32),
            pltpu.VMEM((8, dim), F32),
            pltpu.VMEM((8, dim), F32),
            pltpu.VMEM((8, 256), F32),
            pltpu.VMEM((8, dim), F32),
            pltpu.VMEM((16, 256), F32),
            pltpu.VMEM((4, 16, 256), F32),
            pltpu.VMEM((2 + zs, 4, 16, 256), F32),
            sem((3,)),
            sem((2, 4)),
            sem((2 + zs,)),
            sem((2 + zs,)),
            sem((n,)),
        ]
        + [sem((n, zs))] * 6
        + [sem((n, 5))] * 2
        + [sem((parts, 2))] * 2
        + [sem((parts, 3))] * 2
        + [sem((parts, zs))] * 2
        + [sem((1,))],
        compiler_params=pltpu.CompilerParams(
            collective_id=0, has_side_effects=True, vmem_limit_bytes=61 * 1024 * 1024
        ),
        name="block",
    )(tokens, cot, mask, *biases, *vectors, *weights)[:9]


def finish_kernel(n, *refs):
    big, sums, big_out, refs = refs[:n], refs[n], refs[n + 1 : 2 * n + 1], refs[2 * n + 1 :]
    biases, vectors, held, (in_sem, out_sem) = refs[:3], refs[3:9], refs[9 : 9 + n], refs[9 + n :]
    reads = [pltpu.make_async_copy(big[i], held[i], in_sem.at[i]) for i in range(n)]
    copies = [pltpu.make_async_copy(held[i], big_out[i], out_sem.at[i]) for i in range(n)]
    for read in reads:
        read.start()
    for read, copy in zip(reads, copies):
        read.wait()
        copy.start()
    dp, tn = lax.axis_index("dp"), lax.axis_index("tensor")
    here = sums[tn]

    def at_lane(rows, lane):
        return pltpu.roll(rows, lax.rem(256 - lane, 256), 1)

    heads, w = biases[0].shape
    for h in range(heads):
        moved = at_lane(here, h * HD + dp * w)
        biases[0][h : h + 1, :] = moved[0:1, :w]
        biases[1][h : h + 1, :] = moved[1:2, :w]
    w = biases[2].shape[1]
    for odd in range(2):
        moved = at_lane(here, 128 * odd + dp * w)
        for i in range(4):
            biases[2][2 * i + odd : 2 * i + odd + 1, :] = moved[2 + i : 3 + i, :w]
    for i in range(6):
        w = vectors[i].shape[1]
        slab = sums[i // 2]
        lane = dp * w
        first = 6 + 4 * (i % 2)
        moved = at_lane(slab, lane % 256)
        rows = lax.broadcasted_iota(jnp.int32, moved.shape, 0)
        row = jnp.sum(jnp.where(rows == first + lane // 256, moved, 0.0), axis=0, keepdims=True)
        vectors[i][...] = row[:, :w]
    for copy in copies:
        copy.wait()


def finish(big, sums, like):
    n = len(big)
    vmem, hbm = pl.BlockSpec(memory_space=pltpu.VMEM), pl.BlockSpec(memory_space=pl.ANY)
    return pl.pallas_call(
        functools.partial(finish_kernel, n),
        out_shape=[jax.ShapeDtypeStruct(a.shape, a.dtype) for a in (*big, *like)],
        in_specs=[hbm] * n + [vmem],
        out_specs=[hbm] * n + [vmem] * len(like),
        scratch_shapes=[pltpu.VMEM(a.shape, a.dtype) for a in big] + [pltpu.SemaphoreType.DMA((n,))] * 2,
        name="finish",
    )(*big, sums)


def on_device(
    tokens,
    cotangent,
    image_mask,
    query_weight,
    key_weight,
    value_weight,
    out_weight,
    up_weight,
    down_weight,
    query_bias,
    value_bias,
    up_bias,
    attn_gain,
    attn_shift,
    mlp_gain,
    mlp_shift,
    out_bias,
    down_bias,
):
    zs = lax.axis_size("dp") // 2
    biases = (query_bias, value_bias, up_bias)
    vectors = tuple(v.reshape(1, -1) for v in (attn_gain, attn_shift, mlp_gain, mlp_shift, out_bias, down_bias))
    weights = (query_weight, key_weight, value_weight, out_weight, up_weight, down_weight)
    *grads, sums = block(tokens, cotangent, image_mask, biases, vectors, weights, zs)
    done = finish(grads, sums, biases + vectors)
    return tuple(done[:11]) + tuple(v.reshape(-1) for v in done[11:])


def solution(mesh):
    wide, tall = P("dp", "tensor"), P("tensor", "dp")
    rows = P(("dp", "tensor"), None)
    weights = (wide, wide, wide, tall, wide, tall, tall, tall, tall)
    vectors = (P("dp"),) * 6
    return jax.shard_map(
        on_device,
        mesh=mesh,
        in_specs=(rows, rows, P("dp")) + weights + vectors,
        out_specs=(rows, rows) + weights + vectors,
        check_vma=False,
    )
```

```python
import functools
import math

import jax
import jax.numpy as jnp
from jax import lax
from jax.experimental import pallas as pl
from jax.experimental.pallas import tpu as pltpu
from jax.sharding import PartitionSpec as P

HD = 64
EPS = 1e-05
SLOPE = 1.702
MESH = pl.DeviceIdType.MESH
BF = jnp.bfloat16
F32 = jnp.float32


def coords(zs):
    dp, tn = lax.axis_index("dp"), lax.axis_index("tensor")
    z, y = dp // 2, dp % 2
    x, c = tn // 2, tn % 2
    over_y = (dp + 1 - 2 * y, tn)
    over_x = (dp, tn + 2 - 4 * x)
    first = (dp + (1 - c) * (1 - 2 * y), tn + c * (2 - 4 * x))
    second = (dp + c * (1 - 2 * y), tn + (1 - c) * (2 - 4 * x))
    sibling = (dp, tn + 1 - 2 * c)
    del over_y, over_x
    fx, fy = x + c * (1 - 2 * x), y + (1 - c) * (1 - 2 * y)
    sx, sy = x + (1 - c) * (1 - 2 * x), y + c * (1 - 2 * y)
    return dict(
        dp=dp, tn=tn, z=z, y=y, x=x, c=c, first=first, second=second, sibling=sibling,
        fx=fx, fy=fy, sx=sx, sy=sy, zs=zs,
    )


def z_peer(at, step):
    return (lax.rem(at["z"] + step, at["zs"]) * 2 + at["y"], at["tn"])


def enter(at):
    barrier = pltpu.get_barrier_semaphore()
    peers = [at["first"], at["second"], at["sibling"]]
    for peer in peers:
        pl.semaphore_signal(barrier, inc=1, device_id=peer, device_id_type=MESH)

    @pl.loop(1, at["zs"])
    def _(step):
        pl.semaphore_signal(barrier, inc=1, device_id=z_peer(at, step), device_id_type=MESH)


def entered(at):
    pl.semaphore_wait(pltpu.get_barrier_semaphore(), 3 + at["zs"] - 1)


def remote(src, dst, send, recv, peer):
    return pltpu.make_async_remote_copy(
        src_ref=src, dst_ref=dst, send_sem=send, recv_sem=recv, device_id=peer, device_id_type=MESH
    )


class Gather:
    def __init__(self, at, own, bufs, late, sems):
        self.at, self.own, self.bufs, self.late = at, own, bufs, late
        (self.local, self.zsend, self.zrecv, self.fsend, self.frecv, self.ssend, self.srecv, self.psend, self.precv, self.ysend, self.yrecv) = sems

    def place(self, k):
        at = self.at
        return pltpu.make_async_copy(
            self.own[k], self.bufs[k].at[at["x"], at["c"], at["z"], at["y"]], self.local.at[k]
        )

    def source(self, step):
        at = self.at
        return lax.rem(at["z"] - step + at["zs"], at["zs"])

    def along_z(self, k, step, z):
        at = self.at
        dst = self.bufs[k].at[at["x"], at["c"], z, at["y"]]
        return remote(self.own[k], dst, self.zsend.at[k, step], self.zrecv.at[k, step], z_peer(at, step))

    def block(self, k, step, second, x, y):
        at = self.at
        ref = self.bufs[k].at[x, at["c"], self.source(step), y]
        src = self.own[k] if isinstance(step, int) and step == 0 else ref
        if second:
            return remote(src, ref, self.ssend.at[k, step], self.srecv.at[k, step], at["second"])
        return remote(src, ref, self.fsend.at[k, step], self.frecv.at[k, step], at["first"])

    def line(self, k, kind, x, c, y):
        at = self.at
        ref = self.bufs[k].at[x, c, :, y]
        peer = at["second"] if kind == 0 else at["sibling"]
        return remote(ref, ref, self.psend.at[k, kind], self.precv.at[k, kind], peer)

    def places(self):
        at = self.at
        x, y = at["x"], at["y"]
        return (x, y), (at["fx"], at["fy"]), (at["sx"], at["sy"]), (1 - x, 1 - y)

    def start_own(self, k):
        me = self.places()[0]
        self.block(k, 0, False, *me).start()
        self.block(k, 0, True, *me).start()

    def start_z(self, k):
        self.place(k).start()

        @pl.loop(1, self.at["zs"])
        def _(step):
            self.along_z(k, step, self.at["z"]).start()

    def along_z_first(self, k, step, z):
        at = self.at
        x, y = self.places()[1]
        src, dst = self.bufs[k].at[x, at["c"], at["z"], y], self.bufs[k].at[x, at["c"], z, y]
        return remote(src, dst, self.ysend.at[k, step], self.yrecv.at[k, step], z_peer(at, step))

    def pass_z(self, k):
        self.block(k, 0, False, *self.places()[1]).wait_recv()

        @pl.loop(1, self.at["zs"])
        def _(step):
            self.along_z_first(k, step, self.at["z"]).start()

    def after_z(self, k):
        me = self.places()[0]

        @pl.loop(1, self.at["zs"])
        def _(step):
            self.along_z(k, step, self.source(step)).wait_recv()
            if k not in self.late:
                self.block(k, step, False, *me).start()
            self.block(k, step, True, *me).start()

        self.place(k).wait()
        self.line(k, 1, me[0], self.at["c"], me[1]).start()

    def after_first(self, k):
        first = self.places()[1]
        if k not in self.late:
            self.block(k, 0, False, *first).wait_recv()

        @pl.loop(1, self.at["zs"])
        def _(step):
            if k in self.late:
                self.along_z_first(k, step, self.source(step)).wait_recv()
            else:
                self.block(k, step, False, *first).wait_recv()

        self.line(k, 0, first[0], self.at["c"], first[1]).start()
        self.line(k, 2, first[0], self.at["c"], first[1]).start()

    def after_second(self, k):
        second = self.places()[2]
        c = self.at["c"]
        self.block(k, 0, True, *second).wait_recv()

        @pl.loop(1, self.at["zs"])
        def _(step):
            self.block(k, step, True, *second).wait_recv()

        self.line(k, 3, second[0], c, second[1]).start()

    def after_across(self, k):
        across = self.places()[3]
        c = self.at["c"]
        self.line(k, 0, across[0], c, across[1]).wait_recv()
        self.line(k, 4, across[0], c, across[1]).start()

    def done(self, k):
        me, first, second, across = self.places()
        c = 1 - self.at["c"]
        for kind, (x, y) in ((1, me), (2, second), (3, first), (4, across)):
            self.line(k, kind, x, c, y).wait_recv()

    def drain(self, k):
        me, first, second, across = self.places()
        c = self.at["c"]
        self.block(k, 0, False, *me).wait_send()
        self.block(k, 0, True, *me).wait_send()

        @pl.loop(1, self.at["zs"])
        def _(step):
            self.along_z(k, step, self.at["z"]).wait_send()
            if k in self.late:
                self.along_z_first(k, step, self.at["z"]).wait_send()
            else:
                self.block(k, step, False, *me).wait_send()
            self.block(k, step, True, *me).wait_send()

        self.line(k, 0, first[0], c, first[1]).wait_send()
        for kind, (x, y) in ((1, me), (2, first), (3, second), (4, across)):
            self.line(k, kind, x, c, y).wait_send()


def dg(left, right, dims):
    return lax.dot_general(left, right, dims, preferred_element_type=F32)


NN = (((1,), (0,)), ((), ()))
NT = (((1,), (1,)), ((), ()))
TN = (((0,), (0,)), ((), ()))
CHUNK = 64


def by_rows(rows, body):
    whole = rows // CHUNK

    @pl.loop(0, whole)
    def _(i):
        body(pl.ds(pl.multiple_of(i * CHUNK, CHUNK), CHUNK))

    if rows % CHUNK:
        body(pl.ds(whole * CHUNK, rows % CHUNK))


def norm_parts(values):
    centre = values - jnp.mean(values, axis=-1, keepdims=True)
    inverse = lax.rsqrt(jnp.mean(centre * centre, axis=-1, keepdims=True) + EPS)
    return centre * inverse, inverse


def attend_pair(p, q, k, v, mixed, log):
    cols = pl.ds(pl.multiple_of(p * 2 * HD, 2 * HD), 2 * HD)
    lane = lax.broadcasted_iota(jnp.int32, (1, 2 * HD), 1)
    scale = BF(1.0 / math.sqrt(HD))
    qp, kp, vp = q[:, cols], k[:, cols], v[:, cols]
    outs = []
    for h in range(2):
        qm = jnp.where(lane // HD == h, qp * scale, BF(0))
        scores = dg(kp, qm, NT)
        highest = jnp.max(scores, axis=0, keepdims=True)
        expo = jnp.exp(scores - highest)
        total = jnp.sum(expo, axis=0, keepdims=True)
        probs = (expo * (1.0 / total)).astype(BF)
        outs.append(dg(probs, vp, TN))
        log[p, h : h + 1, :] = highest + jnp.log(total)
    mixed[:, cols] = jnp.where(lane < HD, outs[0], outs[1]).astype(BF)


def place_vectors(at, biases, vectors, own, pad, long, slab):
    query_bias, value_bias, up_bias = biases
    dp = at["dp"]
    heads, w = query_bias.shape
    pad[...] = jnp.zeros_like(pad)
    sums = jnp.zeros(pad.shape, F32)
    for h in range(heads):
        pad[0:1, :w] = query_bias[h : h + 1, :]
        pad[1:2, :w] = value_bias[h : h + 1, :]
        sums += pltpu.roll(pad[...], h * HD + dp * w, 1)
    pad[...] = jnp.zeros_like(pad)
    w = up_bias.shape[1]
    for odd in range(2):
        for i in range(4):
            pad[2 + i : 3 + i, :w] = up_bias[2 * i + odd : 2 * i + odd + 1, :]
        sums += pltpu.roll(pad[...], 128 * odd + dp * w, 1)
    slab[0:8, :] = sums
    slab[8:16, :] = jnp.zeros((8, 256), F32)
    long[...] = jnp.zeros_like(long)
    for i, vector in enumerate(vectors):
        long[i : i + 1, : vector.shape[1]] = vector[...]
    long[...] = pltpu.roll(long[...], dp * vectors[0].shape[1], 1)
    for pair in range(2):
        for i in range(4):
            row = 6 + 4 * pair + i
            slab[row : row + 1, :] = long[pl.ds(2 * at["tn"] + pair, 1), i * 256 : (i + 1) * 256]
    own[...] = slab[...].astype(BF)


class Scatter:
    def __init__(self, at, kept, rs, rf, rz, stage, near, sems):
        self.near = near
        self.at, self.kept, self.rs, self.rf, self.rz, self.stage = at, kept, rs, rf, rz, stage
        self.csend, self.crecv, self.psend, self.precv, self.zsend, self.zrecv, self.local = sems

    def places(self):
        at = self.at
        x, y = at["x"], at["y"]
        return (x, y), (at["fx"], at["fy"]), (at["sx"], at["sy"]), (1 - x, 1 - y)

    def to_sibling(self, k, x, src):
        return remote(src, self.kept[k].at[x], self.csend.at[k, x], self.crecv.at[k, x], self.at["sibling"])

    def to_second(self, k, which):
        x, y = self.places()[2 + which]
        src = self.kept[k].at[x, :, y]
        return remote(src, self.rs[k].at[which], self.psend.at[k, which], self.precv.at[k, which], self.at["second"])

    def to_first(self, k):
        x, y = self.places()[1]
        src = self.kept[k].at[x, :, y]
        return remote(src, self.rf[k], self.psend.at[k, 2], self.precv.at[k, 2], self.at["first"])

    def along_z(self, k, step):
        at = self.at
        src = self.kept[k].at[at["x"], lax.rem(at["z"] + step, at["zs"]), at["y"]]
        return remote(src, self.rz[k].at[step - 1], self.zsend.at[k, step], self.zrecv.at[k, step], z_peer(at, step))

    def fetch(self, k, which):
        return pltpu.make_async_copy(self.rs[k].at[which], self.staged(k, which), self.local.at[0])

    def terms(self, k, which):
        if k in self.near:
            return self.rs[k].at[which]
        self.fetch(k, which).start()
        self.fetch(k, which).wait()
        return self.staged(k, which)

    def staged(self, k, which):
        return self.stage.at[:, :, pl.ds(0, self.kept[k].shape[-1])]

    def start(self, k):
        self.to_second(k, 1).start()
        self.to_second(k, 0).start()

    def add(self, k, place, ref):
        x, y = place

        @pl.loop(0, self.at["zs"])
        def _(i):
            self.kept[k][x, i, y] += ref[i]

    def pass_on(self, k):
        self.to_second(k, 1).wait_recv()
        self.add(k, self.places()[1], self.terms(k, 1))
        self.to_first(k).start()

    def after_second(self, k):
        self.to_second(k, 0).wait_recv()
        self.add(k, self.places()[0], self.terms(k, 0))

    def after_first(self, k):
        self.to_first(k).wait_recv()
        self.add(k, self.places()[0], self.rf[k])

        @pl.loop(1, self.at["zs"])
        def _(step):
            self.along_z(k, step).start()

    def total(self, k):
        at = self.at

        @pl.loop(1, at["zs"])
        def _(step):
            self.along_z(k, step).wait_recv()

        width = self.kept[k].shape[-1]
        others = self.stage.at[pl.ds(0, at["zs"] - 1), :, pl.ds(0, width)]
        fetch = pltpu.make_async_copy(self.rz[k], others, self.local.at[0])
        fetch.start()
        fetch.wait()
        out = self.kept[k][at["x"], at["z"], at["y"]].astype(F32)
        return lax.fori_loop(0, at["zs"] - 1, lambda i, sums: sums + self.stage[i, :, :width].astype(F32), out)

    def drain(self, k):
        self.to_second(k, 0).wait_send()
        self.to_second(k, 1).wait_send()
        self.to_first(k).wait_send()

        @pl.loop(1, self.at["zs"])
        def _(step):
            self.along_z(k, step).wait_send()


def spans(pumps, pump, body):
    def run(first, last):
        @pl.loop(first, last)
        def _(i):
            body(i)

    start = 0
    for i, count in enumerate(pumps):
        if count or i == len(pumps) - 1:
            run(start, i + 1)
            pump(count)
            start = i + 1


def attend_pair_back(p, q, k, v, grad, log):
    cols = pl.ds(pl.multiple_of(p * 2 * HD, 2 * HD), 2 * HD)
    lane = lax.broadcasted_iota(jnp.int32, (1, 2 * HD), 1)
    scale = BF(1.0 / math.sqrt(HD))
    qp, kp, vp, gp = q[:, cols], k[:, cols], v[:, cols], grad[:, cols]
    gq = gk = gv = 0.0
    for h in range(2):
        on = lane // HD == h
        qm = jnp.where(on, qp * scale, BF(0))
        km = jnp.where(on, kp * scale, BF(0))
        gm = jnp.where(on, gp, BF(0))
        probs = jnp.exp(dg(kp, qm, NT) - log[p, h : h + 1, :])
        gv += dg(probs.astype(BF), gm, NN)
        grad_probs = dg(vp, gm, NT)
        inner = jnp.sum(probs * grad_probs, axis=0, keepdims=True)
        grad_scores = (probs * (grad_probs - inner)).astype(BF)
        gk += dg(grad_scores, qm, NN)
        gq += dg(grad_scores, km, TN)
    q[:, cols] = gq.astype(BF)
    k[:, cols] = gk.astype(BF)
    v[:, cols] = gv.astype(BF)


N_OWN = 9
N_PART = 8
LATE = ()
ORDER = [
    ("Z", 0), ("F", 0), ("S", 0), ("Z", 1), ("T", 0), ("D", 0), ("Z", 2), ("F", 1), ("S", 1), ("Z", 3),
    ("F", 2), ("S", 2), ("Z", 4), ("F", 3), ("T", 1), ("D", 1), ("S", 3), ("F", 4), ("Z", 5), ("T", 2),
    ("D", 2), ("S", 4), ("F", 5), ("Z", 6), ("T", 3), ("D", 3), ("T", 4), ("F", 6), ("D", 4), ("Z", 7),
    ("S", 5), ("F", 7), ("Z", 8), ("T", 5), ("D", 5), ("S", 6), ("F", 8), ("T", 6), ("s", 0), ("S", 7),
    ("D", 6), ("T", 7), ("S", 8), ("s", 1), ("D", 7), ("T", 8), ("D", 8), ("a", 0), ("b", 0), ("a", 1),
    ("e", 0), ("b", 1), ("e", 1), ("a", 2), ("f", 0), ("b", 2), ("f", 1), ("e", 2), ("a", 3), ("b", 3),
    ("f", 2), ("a", 4), ("e", 3), ("b", 4), ("e", 4), ("a", 5), ("b", 5), ("f", 3), ("a", 6), ("e", 5),
    ("f", 4), ("b", 6), ("a", 7), ("f", 5), ("e", 6), ("b", 7), ("e", 7), ("f", 6), ("f", 7),
]
PUMPS = {
    "LN1": 1,
    "q": (0, 0, 0, 1),
    "k": (0, 0, 0, 1),
    "v": (0, 0, 0, 0),
    "att": (1, 0, 2, 1, 1, 0, 0, 0),
    "out": 0,
    "LN2": 0,
    "up": ((0, 0, 1, 0), (0, 0, 0, 0)),
    "dn": ((1, 0, 1, 0), (0, 0, 0, 1)),
    "grad": (3, 3, 2, 1, 1, 2, 1, 2),
    "up_back": ((0, 1), (0, 0)),
    "LN2_back": 2,
    "att_back": (1, 0, 3, 0, 0, 0, 1, 3),
    "qk_back": (2, 1, 1, 0),
    "v_back": (0, 0),
    "LN1_back": 3,
    "swap": (1, 0, 1),
}


def block_kernel(zs, tokens_in, cot, mask, *refs):
    n, parts = N_OWN, N_PART
    refs = list(refs)

    def take(count):
        got = refs[:count]
        del refs[:count]
        return got if count > 1 else got[0]

    biases, vectors = take(3), take(6)
    wq, wk, wv, wo, wu, wd = take(6)
    block_out, tokens_grad, gq_out, gk_out, gv_out, go_out, gu_out, gd_out, small_out = take(9)
    bufs, rs, rz = take(n), take(4), take(parts)
    weights = bufs[1:]
    own = take(n)
    kept, rf = take(parts), take(parts)
    rs = rs + take(4)
    (send, stage, wt, pair, grad_out, attn_in, q, k, v, log, mixed, middle, mlp_in, hidden, grad_pre, acc) = take(16)
    vstage, vecs, dvec, dsum, pad, long, slab, small, small_in = take(9)
    load_sem, wt_sem, vsend, vrecv = take(4)
    gsems, ssems = take(11), take(7)
    tokens, grad_mixed, grad_attn = pair.at[0], pair.at[0], pair.at[1]
    rows, dim = attn_in.shape
    hw = wq.shape[1]
    half = wu.shape[1] // 2
    at = coords(zs)
    c = at["c"]
    g = Gather(at, own, bufs, LATE, gsems)
    s = Scatter(at, kept, rs, rf, rz, stage, range(4, parts), ssems)
    w_q, w_k, w_v, w_o, w_u0, w_u1, w_d0, w_d1 = weights

    enter(at)
    load_tokens = pltpu.make_async_copy(tokens_in, tokens, load_sem.at[0])
    load_cot = pltpu.make_async_copy(cot, grad_out, load_sem.at[1])
    load_tokens.start()
    load_cot.start()
    place_vectors(at, biases, vectors, own[0], pad, long, slab)
    own[1][...] = wq[...].astype(BF)
    own[2][...] = wk[...].astype(BF)
    entered(at)

    for i in range(3):
        g.start_z(i)
        g.start_own(i)
    own[3][...] = wv[...].astype(BF)
    own[4][...] = wo[...].T.astype(BF)
    g.start_own(3)
    g.start_own(4)
    own[5][...] = wu[:, :half].astype(BF)
    own[6][...] = wu[:, half:].astype(BF)
    own[7][...] = wd[:half, :].T.astype(BF)
    own[8][...] = wd[half:, :].T.astype(BF)

    def after_z(i):
        if i + 2 < n and i > 0:
            g.start_z(i + 2)
            if i + 2 >= 5:
                g.start_own(i + 2)
        g.after_z(i)

    def finish_part(i):
        sums = s.total(i)
        if i < 2:
            gd_out[i * half : (i + 1) * half, :] = sums.T
        elif i < 4:
            gu_out[:, (i - 2) * half : (i - 1) * half] = sums
        elif i == 4:
            go_out[...] = sums.T
        else:
            (gv_out, gq_out, gk_out)[i - 5][...] = sums

    kinds = {
        "X": g.pass_z, "Z": after_z, "F": g.after_first, "S": g.after_second, "T": g.after_across, "D": g.done,
        "s": s.start, "a": s.pass_on, "b": s.after_second, "e": s.after_first, "f": finish_part,
    }
    steps = list(reversed(ORDER))

    def take_step():
        what, i = steps.pop()
        kinds[what](i)

    def pump(count=1):
        for _ in range(min(count, len(steps))):
            take_step()

    def until(what, i):
        while (what, i) in steps:
            take_step()

    def tile_copy(w, t, side=0, part=0):
        width = w.shape[-1]
        dst = wt.at[t, :, :, :, pl.ds(side * hw, width)]
        return pltpu.make_async_copy(w.at[t // 2, t % 2], dst, wt_sem.at[part, t])

    def fetch(w, side=0, part=0):
        for t in range(4):
            tile_copy(w, t, side, part).start()

    def tile(w, t, side=0, part=0):
        tile_copy(w, t, side, part).wait()
        return wt[t, :, :, :, side * hw : side * hw + w.shape[-1]].reshape(dim, -1)

    def tiles(w, pumps, body):
        spans(pumps, pump, lambda t: body(t, tile(w, t)))

    def columns(t):
        return pl.ds(pl.multiple_of(t * hw, hw), hw)

    def product(i, make):
        slot = i % 2
        width = kept[i].shape[-1]

        def out(x):
            return send.at[slot, x, :, :, :, pl.ds(0, width)]

        if i >= 2:
            for x in range(2):
                before = send.at[slot, x, :, :, :, pl.ds(0, kept[i - 2].shape[-1])]
                s.to_sibling(i - 2, x, before).wait_send()

        @pl.loop(0, 2)
        def _(x):
            send[slot, x, :, :, :, :width] = make(2 * x + 1 - c).astype(BF).reshape(kept[i].shape[1:])
            s.to_sibling(i, x, out(x)).start()

        @pl.loop(0, 2)
        def _(x):
            terms = make(2 * x + c)
            s.to_sibling(i, x, out(x)).wait_recv()
            other = kept[i][x].reshape(dim, -1).astype(F32)
            kept[i][x] = (terms + other).astype(BF).reshape(kept[i].shape[1:])

        if i >= 2:
            s.start(i)
        pump(PUMPS["grad"][i])

    until("D", 0)
    for t in range(4):
        fetch_vectors = pltpu.make_async_copy(bufs[0].at[t // 2, t % 2], vstage, load_sem.at[2])
        fetch_vectors.start()
        fetch_vectors.wait()
        vecs[t] = jnp.sum(vstage[...].astype(F32).reshape(-1, 16, 256), axis=0)
    for t in range(3):
        for which in range(2):
            first = 6 + 4 * which
            dvec[2 * t + which : 2 * t + which + 1, :] = jnp.concatenate(
                [vecs[t, first + i : first + i + 1, :] for i in range(4)], axis=1
            )
    keep = mask[at["tn"]].astype(F32)
    load_tokens.wait()
    load_cot.wait()

    def norm_a(sl):
        grad_out[sl, :] = (grad_out[sl, :].astype(F32) * keep).astype(BF)
        normed, _ = norm_parts(tokens[sl, :].astype(F32))
        attn_in[sl, :] = (normed * dvec[0:1, :] + dvec[1:2, :]).astype(BF)

    by_rows(rows, norm_a)
    pump(PUMPS["LN1"])

    def project(dst, bias_row):
        def body(t, w):
            got = dg(attn_in[...], w, NN)
            if bias_row is not None:
                got = got + vecs[t, bias_row : bias_row + 1, :]
            dst[:, columns(t)] = got.astype(BF)

        return body

    for i, (w, dst, bias_row, name) in enumerate(((w_q, q, 0, "q"), (w_k, k, None, "k"), (w_v, v, 1, "v"))):
        until("D", 1 + i)
        fetch(w)
        tiles(w, PUMPS[name], project(dst, bias_row))
    spans(PUMPS["att"], pump, lambda p: attend_pair(p, q, k, v, mixed, log))
    until("D", 4)
    fetch(w_o)
    acc[...] = jnp.zeros_like(acc)

    def out_project(i):
        two = [dg(mixed[:, columns(t)], tile(w_o, t), NT) for t in (2 * i, 2 * i + 1)]
        acc[...] += two[0] + two[1]

    spans((0, PUMPS["out"]), pump, out_project)

    def norm_m(sl):
        mid = tokens[sl, :].astype(F32) + acc[sl, :] + dvec[4:5, :]
        middle[sl, :] = mid
        normed, _ = norm_parts(mid)
        mlp_in[sl, :] = (normed * dvec[2:3, :] + dvec[3:4, :]).astype(BF)

    by_rows(rows, norm_m)
    pump(PUMPS["LN2"])

    def hidden_of(which, t):
        if which == 0:
            return hidden.at[t]
        return pair.at[t // 2, :, pl.ds(pl.multiple_of(t % 2 * half, half), half)]

    def up(which):
        def body(t, w):
            bias = jnp.concatenate(
                [vecs[t, 2 + 2 * which + i : 3 + 2 * which + i, :] for i in range(2)], axis=1
            )
            pre = dg(mlp_in[...], w, NN) + bias
            sigma = 0.5 + 0.5 * jnp.tanh((0.5 * SLOPE) * pre)
            hid = pre * sigma
            hidden_of(which, t)[...] = hid.astype(BF)
            grad_pre[which * 4 + t] = (sigma + SLOPE * hid * (1.0 - sigma)).astype(BF)

        return body

    for which, w in enumerate((w_u0, w_u1)):
        until("D", 5 + which)
        fetch(w)
        tiles(w, PUMPS["up"][which], up(which))
        if which == 0:
            product(0, lambda t: dg(grad_out[...], hidden_of(0, t)[...], TN))
    product(1, lambda t: dg(grad_out[...], hidden_of(1, t)[...], TN))
    acc[...] = jnp.zeros_like(acc)

    def down(which):
        def body(t, w):
            j = which * 4 + t
            acc[...] += dg(hidden_of(which, t)[...], w, NT)
            grad_hidden = dg(grad_out[...], w, NN)
            grad_pre[j] = (grad_hidden * grad_pre[j].astype(F32)).astype(BF)

        return body

    def up_terms(which):
        return lambda t: dg(mlp_in[...], grad_pre[which * 4 + t], TN)

    until("D", 7)
    fetch(w_d0)
    tiles(w_d0, PUMPS["dn"][0], down(0))
    product(2, up_terms(0))
    until("D", 8)
    fetch(w_d1)
    tiles(w_d1, PUMPS["dn"][1], down(1))
    fetch(w_u0)

    def finish_rows(sl):
        pair[0, sl, :] = ((middle[sl, :] + acc[sl, :] + dvec[5:6, :]) * keep).astype(BF)

    by_rows(rows, finish_rows)
    store_block = pltpu.make_async_copy(pair.at[0], block_out, load_sem.at[2])
    store_block.start()

    product(3, up_terms(1))

    def up_back(which):
        def body(i):
            w = w_u1 if which else w_u0
            two = [dg(grad_pre[which * 4 + t], tile(w, t), NT) for t in (2 * i, 2 * i + 1)]
            acc[...] += two[0] + two[1]

        return body

    acc[...] = jnp.zeros_like(acc)
    spans(PUMPS["up_back"][0], pump, up_back(0))
    fetch(w_u1)
    spans(PUMPS["up_back"][1], pump, up_back(1))
    fetch(w_o)
    dsum[...] = jnp.zeros_like(dsum)

    def norm_back(values, grad, gain, at_row):
        normed, inverse = norm_parts(values)
        scaled = grad * gain
        dsum[at_row : at_row + 1, :] += jnp.sum(grad * normed, axis=0, keepdims=True)
        dsum[at_row + 1 : at_row + 2, :] += jnp.sum(grad, axis=0, keepdims=True)
        return inverse * (
            scaled
            - jnp.mean(scaled, axis=-1, keepdims=True)
            - normed * jnp.mean(scaled * normed, axis=-1, keepdims=True)
        )

    def norm_m_back(sl):
        through = grad_out[sl, :].astype(F32)
        grad = through + norm_back(middle[sl, :], acc[sl, :], dvec[2:3, :], 2)
        dsum[4:5, :] += jnp.sum(grad, axis=0, keepdims=True)
        dsum[5:6, :] += jnp.sum(through, axis=0, keepdims=True)
        middle[sl, :] = grad
        grad_attn[sl, :] = grad.astype(BF)

    by_rows(rows, norm_m_back)
    store_block.wait()
    pump(PUMPS["LN2_back"])

    def mixed_back(t, w):
        grad_mixed[:, columns(t)] = dg(grad_attn[...], w, NN).astype(BF)

    tiles(w_o, (0, 0, 0, 0), mixed_back)
    product(4, lambda t: dg(grad_attn[...], mixed[:, columns(t)], TN))
    fetch(w_q, 0, 0)
    fetch(w_k, 1, 1)
    spans(PUMPS["att_back"], pump, lambda p: attend_pair_back(p, q, k, v, grad_mixed, log))
    reload_tokens = pltpu.make_async_copy(tokens_in, tokens, load_sem.at[0])
    reload_tokens.start()
    for i, grad in ((5, v), (6, q), (7, k)):
        product(i, lambda t, grad=grad: dg(attn_in[...], grad[:, columns(t)], TN))
    for t in range(4):
        cols = slice(t * hw, (t + 1) * hw)
        small[t, 0:1, :] = jnp.sum(q[:, cols].astype(F32), axis=0, keepdims=True)
        small[t, 1:2, :] = jnp.sum(v[:, cols].astype(F32), axis=0, keepdims=True)
        for which in range(2):
            sums = jnp.sum(grad_pre[which * 4 + t].astype(F32), axis=0, keepdims=True)
            for i in range(2):
                row = 2 + 2 * which + i
                small[t, row : row + 1, :] = sums[:, i * 256 : (i + 1) * 256]
        small[t, 6:16, :] = jnp.zeros((10, 256), F32)
    acc[...] = jnp.zeros_like(acc)

    def qk_back(t):
        tile_copy(w_q, t, 0, 0).wait()
        tile_copy(w_k, t, 1, 1).wait()
        both = jnp.concatenate([q[:, columns(t)], k[:, columns(t)]], axis=1)
        acc[...] += dg(both, wt[t].reshape(dim, -1), NT)

    spans(PUMPS["qk_back"], pump, qk_back)
    fetch(w_v)

    def v_back(i):
        two = [dg(v[:, columns(t)], tile(w_v, t), NT) for t in (2 * i, 2 * i + 1)]
        acc[...] += two[0] + two[1]

    spans(PUMPS["v_back"], pump, v_back)
    reload_tokens.wait()

    def norm_a_back(sl):
        values = tokens[sl, :].astype(F32)
        middle[sl, :] += norm_back(values, acc[sl, :], dvec[0:1, :], 0)

    by_rows(rows, norm_a_back)
    store_grad = pltpu.make_async_copy(middle, tokens_grad, load_sem.at[1])
    store_grad.start()
    pump(PUMPS["LN1_back"])
    for i in range(6):
        for j in range(4):
            row = 6 + 4 * (i % 2) + j
            small[i // 2, row : row + 1, :] = dsum[i : i + 1, j * 256 : (j + 1) * 256]
    x, y = at["x"], at["y"]
    peers = [at["sibling"], (at["dp"], at["tn"] + 2 - 4 * x), (at["dp"] + 1 - 2 * y, at["tn"])]

    def swap(i):
        return remote(small, small_in.at[i], vsend.at[i], vrecv.at[i], peers[i])

    def swap_z(step):
        return remote(small, small_in.at[2 + step], vsend.at[2 + step], vrecv.at[2 + step], z_peer(at, step))

    for i in range(3):
        swap(i).start()
        pump(PUMPS["swap"][i])
        swap(i).wait()
        small[...] += small_in[i]

    @pl.loop(1, zs)
    def _(step):
        swap_z(step).start()

    pump(len(steps))

    @pl.loop(1, zs)
    def _(step):
        swap_z(step).wait()

    small_out[...] = lax.fori_loop(1, zs, lambda step, sums: sums + small_in[2 + step], small[...])
    store_grad.wait()
    for i in range(n):
        g.drain(i)
    for i in range(parts):
        if i >= parts - 2:
            for x_ in range(2):
                out = send.at[i % 2, x_, :, :, :, pl.ds(0, kept[i].shape[-1])]
                s.to_sibling(i, x_, out).wait_send()
        s.drain(i)


def block(tokens, cot, mask, biases, vectors, weights, zs):
    rows, dim = tokens.shape
    wq, wk, wv, wo, wu, wd = weights
    r, hw = wq.shape
    half = wu.shape[1] // 2
    n, parts = N_OWN, N_PART
    vmem, hbm = pl.BlockSpec(memory_space=pltpu.VMEM), pl.BlockSpec(memory_space=pl.ANY)
    shape, sem = jax.ShapeDtypeStruct, pltpu.SemaphoreType.DMA
    own_widths = [hw] * 4 + [half] * 4
    widths = [half] * 4 + [hw] * 4
    outs = [
        shape((rows, dim), BF),
        shape((rows, dim), F32),
        shape((r, hw), F32),
        shape((r, hw), F32),
        shape((r, hw), F32),
        shape((hw, r), F32),
        shape((r, 2 * half), F32),
        shape((2 * half, r), F32),
        shape((4, 16, 256), F32),
    ]
    outs += [shape((2, 2, zs, 2, 16, 256), BF)]
    outs += [shape((2, 2, zs, 2, r, w), BF) for w in own_widths]
    outs += [shape((2, zs, r, w), BF) for w in widths[:4]]
    outs += [shape((zs - 1, r, w), BF) for w in widths]
    act, wide = pltpu.VMEM((rows, dim), BF), pltpu.VMEM((rows, dim), F32)
    return pl.pallas_call(
        functools.partial(block_kernel, zs),
        out_shape=outs,
        in_specs=[hbm, hbm, pl.BlockSpec(memory_space=pltpu.SMEM)] + [vmem] * 15,
        out_specs=[hbm] * 2 + [vmem] * 7 + [hbm] * (n + 4 + parts),
        scratch_shapes=[pltpu.VMEM((16, 256), BF)]
        + [pltpu.VMEM((r, w), BF) for w in own_widths]
        + [pltpu.VMEM((2, zs, 2, r, w), BF) for w in widths]
        + [pltpu.VMEM((zs, r, w), BF) for w in widths]
        + [pltpu.VMEM((2, zs, r, w), BF) for w in widths[4:]]
        + [
            pltpu.VMEM((2, 2, zs, 2, r, half), BF),
            pltpu.VMEM((zs, r, half), BF),
            pltpu.VMEM((4, zs, 2, r, half), BF),
            pltpu.VMEM((2, rows, dim), BF),
            act,
            act,
            act,
            act,
            act,
            pltpu.VMEM((dim // HD // 2, 2, rows), F32),
            act,
            wide,
            act,
            pltpu.VMEM((4, rows, half), BF),
            pltpu.VMEM((8, rows, half), BF),
            wide,
            pltpu.VMEM((zs, 2, 16, 256), BF),
            pltpu.VMEM((4, 16, 256), F32),
            pltpu.VMEM((8, dim), F32),
            pltpu.VMEM((8, dim), F32),
            pltpu.VMEM((8, 256), F32),
            pltpu.VMEM((8, dim), F32),
            pltpu.VMEM((16, 256), F32),
            pltpu.VMEM((4, 16, 256), F32),
            pltpu.VMEM((2 + zs, 4, 16, 256), F32),
            sem((3,)),
            sem((2, 4)),
            sem((2 + zs,)),
            sem((2 + zs,)),
            sem((n,)),
        ]
        + [sem((n, zs))] * 6
        + [sem((n, 5))] * 2
        + [sem((n, zs))] * 2
        + [sem((parts, 2))] * 2
        + [sem((parts, 3))] * 2
        + [sem((parts, zs))] * 2
        + [sem((1,))],
        compiler_params=pltpu.CompilerParams(
            collective_id=0, has_side_effects=True, vmem_limit_bytes=62 * 1024 * 1024
        ),
        name="block",
    )(tokens, cot, mask, *biases, *vectors, *weights)[:9]


def finish_kernel(n, *refs):
    big, sums, big_out, refs = refs[:n], refs[n], refs[n + 1 : 2 * n + 1], refs[2 * n + 1 :]
    biases, vectors, held, (in_sem, out_sem) = refs[:3], refs[3:9], refs[9 : 9 + n], refs[9 + n :]
    reads = [pltpu.make_async_copy(big[i], held[i], in_sem.at[i]) for i in range(n)]
    copies = [pltpu.make_async_copy(held[i], big_out[i], out_sem.at[i]) for i in range(n)]
    for read in reads:
        read.start()
    for read, copy in zip(reads, copies):
        read.wait()
        copy.start()
    dp, tn = lax.axis_index("dp"), lax.axis_index("tensor")
    here = sums[tn]

    def at_lane(rows, lane):
        return pltpu.roll(rows, lax.rem(256 - lane, 256), 1)

    heads, w = biases[0].shape
    for h in range(heads):
        moved = at_lane(here, h * HD + dp * w)
        biases[0][h : h + 1, :] = moved[0:1, :w]
        biases[1][h : h + 1, :] = moved[1:2, :w]
    w = biases[2].shape[1]
    for odd in range(2):
        moved = at_lane(here, 128 * odd + dp * w)
        for i in range(4):
            biases[2][2 * i + odd : 2 * i + odd + 1, :] = moved[2 + i : 3 + i, :w]
    for i in range(6):
        w = vectors[i].shape[1]
        slab = sums[i // 2]
        lane = dp * w
        first = 6 + 4 * (i % 2)
        moved = at_lane(slab, lane % 256)
        rows = lax.broadcasted_iota(jnp.int32, moved.shape, 0)
        row = jnp.sum(jnp.where(rows == first + lane // 256, moved, 0.0), axis=0, keepdims=True)
        vectors[i][...] = row[:, :w]
    for copy in copies:
        copy.wait()


def finish(big, sums, like):
    n = len(big)
    vmem, hbm = pl.BlockSpec(memory_space=pltpu.VMEM), pl.BlockSpec(memory_space=pl.ANY)
    return pl.pallas_call(
        functools.partial(finish_kernel, n),
        out_shape=[jax.ShapeDtypeStruct(a.shape, a.dtype) for a in (*big, *like)],
        in_specs=[hbm] * n + [vmem],
        out_specs=[hbm] * n + [vmem] * len(like),
        scratch_shapes=[pltpu.VMEM(a.shape, a.dtype) for a in big] + [pltpu.SemaphoreType.DMA((n,))] * 2,
        name="finish",
    )(*big, sums)


def on_device(
    tokens,
    cotangent,
    image_mask,
    query_weight,
    key_weight,
    value_weight,
    out_weight,
    up_weight,
    down_weight,
    query_bias,
    value_bias,
    up_bias,
    attn_gain,
    attn_shift,
    mlp_gain,
    mlp_shift,
    out_bias,
    down_bias,
):
    zs = lax.axis_size("dp") // 2
    biases = (query_bias, value_bias, up_bias)
    vectors = tuple(v.reshape(1, -1) for v in (attn_gain, attn_shift, mlp_gain, mlp_shift, out_bias, down_bias))
    weights = (query_weight, key_weight, value_weight, out_weight, up_weight, down_weight)
    *grads, sums = block(tokens, cotangent, image_mask, biases, vectors, weights, zs)
    done = finish(grads, sums, biases + vectors)
    return tuple(done[:11]) + tuple(v.reshape(-1) for v in done[11:])


def solution(mesh):
    wide, tall = P("dp", "tensor"), P("tensor", "dp")
    rows = P(("dp", "tensor"), None)
    weights = (wide, wide, wide, tall, wide, tall, tall, tall, tall)
    vectors = (P("dp"),) * 6
    return jax.shard_map(
        on_device,
        mesh=mesh,
        in_specs=(rows, rows, P("dp")) + weights + vectors,
        out_specs=(rows, rows) + weights + vectors,
        check_vma=False,
    )
```

```python
import functools
import math

import jax
import jax.numpy as jnp
from jax import lax
from jax.experimental import pallas as pl
from jax.experimental.pallas import tpu as pltpu
from jax.sharding import PartitionSpec as P

HD = 64
EPS = 1e-05
SLOPE = 1.702
MESH = pl.DeviceIdType.MESH
BF = jnp.bfloat16
F32 = jnp.float32


def coords(zs):
    dp, tn = lax.axis_index("dp"), lax.axis_index("tensor")
    z, y = dp // 2, dp % 2
    x, c = tn // 2, tn % 2
    over_y = (dp + 1 - 2 * y, tn)
    over_x = (dp, tn + 2 - 4 * x)
    first = (dp + (1 - c) * (1 - 2 * y), tn + c * (2 - 4 * x))
    second = (dp + c * (1 - 2 * y), tn + (1 - c) * (2 - 4 * x))
    sibling = (dp, tn + 1 - 2 * c)
    del over_y, over_x
    fx, fy = x + c * (1 - 2 * x), y + (1 - c) * (1 - 2 * y)
    sx, sy = x + (1 - c) * (1 - 2 * x), y + c * (1 - 2 * y)
    return dict(
        dp=dp, tn=tn, z=z, y=y, x=x, c=c, first=first, second=second, sibling=sibling,
        fx=fx, fy=fy, sx=sx, sy=sy, zs=zs,
    )


def z_peer(at, step):
    return (lax.rem(at["z"] + step, at["zs"]) * 2 + at["y"], at["tn"])


def enter(at):
    barrier = pltpu.get_barrier_semaphore()
    peers = [at["first"], at["second"], at["sibling"]]
    for peer in peers:
        pl.semaphore_signal(barrier, inc=1, device_id=peer, device_id_type=MESH)

    @pl.loop(1, at["zs"])
    def _(step):
        pl.semaphore_signal(barrier, inc=1, device_id=z_peer(at, step), device_id_type=MESH)


def entered(at):
    pl.semaphore_wait(pltpu.get_barrier_semaphore(), 3 + at["zs"] - 1)


def remote(src, dst, send, recv, peer):
    return pltpu.make_async_remote_copy(
        src_ref=src, dst_ref=dst, send_sem=send, recv_sem=recv, device_id=peer, device_id_type=MESH
    )


class Gather:
    def __init__(self, at, own, bufs, late, sems):
        self.at, self.own, self.bufs, self.late = at, own, bufs, late
        (self.local, self.zsend, self.zrecv, self.fsend, self.frecv, self.ssend, self.srecv, self.psend, self.precv, self.ysend, self.yrecv) = sems

    def place(self, k):
        at = self.at
        return pltpu.make_async_copy(
            self.own[k], self.bufs[k].at[at["x"], at["c"], at["z"], at["y"]], self.local.at[k]
        )

    def source(self, step):
        at = self.at
        return lax.rem(at["z"] - step + at["zs"], at["zs"])

    def along_z(self, k, step, z):
        at = self.at
        dst = self.bufs[k].at[at["x"], at["c"], z, at["y"]]
        return remote(self.own[k], dst, self.zsend.at[k, step], self.zrecv.at[k, step], z_peer(at, step))

    def block(self, k, step, second, x, y):
        at = self.at
        ref = self.bufs[k].at[x, at["c"], self.source(step), y]
        src = self.own[k] if isinstance(step, int) and step == 0 else ref
        if second:
            return remote(src, ref, self.ssend.at[k, step], self.srecv.at[k, step], at["second"])
        return remote(src, ref, self.fsend.at[k, step], self.frecv.at[k, step], at["first"])

    def line(self, k, kind, x, c, y):
        at = self.at
        ref = self.bufs[k].at[x, c, :, y]
        peer = at["second"] if kind == 0 else at["sibling"]
        return remote(ref, ref, self.psend.at[k, kind], self.precv.at[k, kind], peer)

    def places(self):
        at = self.at
        x, y = at["x"], at["y"]
        return (x, y), (at["fx"], at["fy"]), (at["sx"], at["sy"]), (1 - x, 1 - y)

    def start_own(self, k):
        me = self.places()[0]
        self.block(k, 0, False, *me).start()
        self.block(k, 0, True, *me).start()

    def start_z(self, k):
        self.place(k).start()

        @pl.loop(1, self.at["zs"])
        def _(step):
            self.along_z(k, step, self.at["z"]).start()

    def along_z_first(self, k, step, z):
        at = self.at
        x, y = self.places()[1]
        src, dst = self.bufs[k].at[x, at["c"], at["z"], y], self.bufs[k].at[x, at["c"], z, y]
        return remote(src, dst, self.ysend.at[k, step], self.yrecv.at[k, step], z_peer(at, step))

    def pass_z(self, k):
        self.block(k, 0, False, *self.places()[1]).wait_recv()

        @pl.loop(1, self.at["zs"])
        def _(step):
            self.along_z_first(k, step, self.at["z"]).start()

    def after_z(self, k):
        me = self.places()[0]

        @pl.loop(1, self.at["zs"])
        def _(step):
            self.along_z(k, step, self.source(step)).wait_recv()
            if k not in self.late:
                self.block(k, step, False, *me).start()
            self.block(k, step, True, *me).start()

        self.place(k).wait()
        self.line(k, 1, me[0], self.at["c"], me[1]).start()

    def after_first(self, k):
        first = self.places()[1]
        if k not in self.late:
            self.block(k, 0, False, *first).wait_recv()

        @pl.loop(1, self.at["zs"])
        def _(step):
            if k in self.late:
                self.along_z_first(k, step, self.source(step)).wait_recv()
            else:
                self.block(k, step, False, *first).wait_recv()

        self.line(k, 0, first[0], self.at["c"], first[1]).start()
        self.line(k, 2, first[0], self.at["c"], first[1]).start()

    def after_second(self, k):
        second = self.places()[2]
        c = self.at["c"]
        self.block(k, 0, True, *second).wait_recv()

        @pl.loop(1, self.at["zs"])
        def _(step):
            self.block(k, step, True, *second).wait_recv()

        self.line(k, 3, second[0], c, second[1]).start()

    def after_across(self, k):
        across = self.places()[3]
        c = self.at["c"]
        self.line(k, 0, across[0], c, across[1]).wait_recv()
        self.line(k, 4, across[0], c, across[1]).start()

    def done(self, k):
        me, first, second, across = self.places()
        c = 1 - self.at["c"]
        for kind, (x, y) in ((1, me), (2, second), (3, first), (4, across)):
            self.line(k, kind, x, c, y).wait_recv()

    def drain(self, k):
        me, first, second, across = self.places()
        c = self.at["c"]
        self.block(k, 0, False, *me).wait_send()
        self.block(k, 0, True, *me).wait_send()

        @pl.loop(1, self.at["zs"])
        def _(step):
            self.along_z(k, step, self.at["z"]).wait_send()
            if k in self.late:
                self.along_z_first(k, step, self.at["z"]).wait_send()
            else:
                self.block(k, step, False, *me).wait_send()
            self.block(k, step, True, *me).wait_send()

        self.line(k, 0, first[0], c, first[1]).wait_send()
        for kind, (x, y) in ((1, me), (2, first), (3, second), (4, across)):
            self.line(k, kind, x, c, y).wait_send()


def dg(left, right, dims):
    return lax.dot_general(left, right, dims, preferred_element_type=F32)


NN = (((1,), (0,)), ((), ()))
NT = (((1,), (1,)), ((), ()))
TN = (((0,), (0,)), ((), ()))
CHUNK = 64


def by_rows(rows, body):
    whole = rows // CHUNK

    @pl.loop(0, whole)
    def _(i):
        body(pl.ds(pl.multiple_of(i * CHUNK, CHUNK), CHUNK))

    if rows % CHUNK:
        body(pl.ds(whole * CHUNK, rows % CHUNK))


def norm_parts(values):
    centre = values - jnp.mean(values, axis=-1, keepdims=True)
    inverse = lax.rsqrt(jnp.mean(centre * centre, axis=-1, keepdims=True) + EPS)
    return centre * inverse, inverse


def attend_pair(p, q, k, v, mixed, log):
    cols = pl.ds(pl.multiple_of(p * 2 * HD, 2 * HD), 2 * HD)
    lane = lax.broadcasted_iota(jnp.int32, (1, 2 * HD), 1)
    scale = BF(1.0 / math.sqrt(HD))
    qp, kp, vp = q[:, cols], k[:, cols], v[:, cols]
    outs = []
    for h in range(2):
        qm = jnp.where(lane // HD == h, qp * scale, BF(0))
        scores = dg(kp, qm, NT)
        highest = jnp.max(scores, axis=0, keepdims=True)
        expo = jnp.exp(scores - highest)
        total = jnp.sum(expo, axis=0, keepdims=True)
        probs = (expo * (1.0 / total)).astype(BF)
        outs.append(dg(probs, vp, TN))
        log[p, h : h + 1, :] = highest + jnp.log(total)
    mixed[:, cols] = jnp.where(lane < HD, outs[0], outs[1]).astype(BF)


def place_vectors(at, biases, vectors, own, pad, long, slab):
    query_bias, value_bias, up_bias = biases
    dp = at["dp"]
    heads, w = query_bias.shape
    pad[...] = jnp.zeros_like(pad)
    sums = jnp.zeros(pad.shape, F32)
    for h in range(heads):
        pad[0:1, :w] = query_bias[h : h + 1, :]
        pad[1:2, :w] = value_bias[h : h + 1, :]
        sums += pltpu.roll(pad[...], h * HD + dp * w, 1)
    pad[...] = jnp.zeros_like(pad)
    w = up_bias.shape[1]
    for odd in range(2):
        for i in range(4):
            pad[2 + i : 3 + i, :w] = up_bias[2 * i + odd : 2 * i + odd + 1, :]
        sums += pltpu.roll(pad[...], 128 * odd + dp * w, 1)
    slab[0:8, :] = sums
    slab[8:16, :] = jnp.zeros((8, 256), F32)
    long[...] = jnp.zeros_like(long)
    for i, vector in enumerate(vectors):
        long[i : i + 1, : vector.shape[1]] = vector[...]
    long[...] = pltpu.roll(long[...], dp * vectors[0].shape[1], 1)
    for pair in range(2):
        for i in range(4):
            row = 6 + 4 * pair + i
            slab[row : row + 1, :] = long[pl.ds(2 * at["tn"] + pair, 1), i * 256 : (i + 1) * 256]
    own[...] = slab[...].astype(BF)


class Scatter:
    def __init__(self, at, kept, rs, rf, rz, stage, near, sems):
        self.near = near
        self.at, self.kept, self.rs, self.rf, self.rz, self.stage = at, kept, rs, rf, rz, stage
        self.csend, self.crecv, self.psend, self.precv, self.zsend, self.zrecv, self.local = sems

    def places(self):
        at = self.at
        x, y = at["x"], at["y"]
        return (x, y), (at["fx"], at["fy"]), (at["sx"], at["sy"]), (1 - x, 1 - y)

    def to_sibling(self, k, x, src):
        return remote(src, self.kept[k].at[x], self.csend.at[k, x], self.crecv.at[k, x], self.at["sibling"])

    def to_second(self, k, which):
        x, y = self.places()[2 + which]
        src = self.kept[k].at[x, :, y]
        return remote(src, self.rs[k].at[which], self.psend.at[k, which], self.precv.at[k, which], self.at["second"])

    def to_first(self, k):
        x, y = self.places()[1]
        src = self.kept[k].at[x, :, y]
        return remote(src, self.rf[k], self.psend.at[k, 2], self.precv.at[k, 2], self.at["first"])

    def along_z(self, k, step):
        at = self.at
        src = self.kept[k].at[at["x"], lax.rem(at["z"] + step, at["zs"]), at["y"]]
        return remote(src, self.rz[k].at[step - 1], self.zsend.at[k, step], self.zrecv.at[k, step], z_peer(at, step))

    def fetch(self, k, which):
        return pltpu.make_async_copy(self.rs[k].at[which], self.staged(k, which), self.local.at[0])

    def terms(self, k, which):
        if k in self.near:
            return self.rs[k].at[which]
        self.fetch(k, which).start()
        self.fetch(k, which).wait()
        return self.staged(k, which)

    def staged(self, k, which):
        return self.stage.at[:, :, pl.ds(0, self.kept[k].shape[-1])]

    def start(self, k):
        self.to_second(k, 1).start()
        self.to_second(k, 0).start()

    def add(self, k, place, ref):
        x, y = place

        @pl.loop(0, self.at["zs"])
        def _(i):
            self.kept[k][x, i, y] += ref[i]

    def pass_on(self, k):
        self.to_second(k, 1).wait_recv()
        self.add(k, self.places()[1], self.terms(k, 1))
        self.to_first(k).start()

    def after_second(self, k):
        self.to_second(k, 0).wait_recv()
        self.add(k, self.places()[0], self.terms(k, 0))

    def after_first(self, k):
        self.to_first(k).wait_recv()
        self.add(k, self.places()[0], self.rf[k])

        @pl.loop(1, self.at["zs"])
        def _(step):
            self.along_z(k, step).start()

    def total(self, k):
        at = self.at

        @pl.loop(1, at["zs"])
        def _(step):
            self.along_z(k, step).wait_recv()

        width = self.kept[k].shape[-1]
        others = self.stage.at[pl.ds(0, at["zs"] - 1), :, pl.ds(0, width)]
        fetch = pltpu.make_async_copy(self.rz[k], others, self.local.at[0])
        fetch.start()
        fetch.wait()
        out = self.kept[k][at["x"], at["z"], at["y"]].astype(F32)
        return lax.fori_loop(0, at["zs"] - 1, lambda i, sums: sums + self.stage[i, :, :width].astype(F32), out)

    def drain(self, k):
        self.to_second(k, 0).wait_send()
        self.to_second(k, 1).wait_send()
        self.to_first(k).wait_send()

        @pl.loop(1, self.at["zs"])
        def _(step):
            self.along_z(k, step).wait_send()


def spans(pumps, pump, body):
    def run(first, last):
        @pl.loop(first, last)
        def _(i):
            body(i)

    start = 0
    for i, count in enumerate(pumps):
        if count or i == len(pumps) - 1:
            run(start, i + 1)
            pump(count)
            start = i + 1


def attend_pair_back(p, q, k, v, grad, log):
    cols = pl.ds(pl.multiple_of(p * 2 * HD, 2 * HD), 2 * HD)
    lane = lax.broadcasted_iota(jnp.int32, (1, 2 * HD), 1)
    scale = BF(1.0 / math.sqrt(HD))
    qp, kp, vp, gp = q[:, cols], k[:, cols], v[:, cols], grad[:, cols]
    gq = gk = gv = 0.0
    for h in range(2):
        on = lane // HD == h
        qm = jnp.where(on, qp * scale, BF(0))
        km = jnp.where(on, kp * scale, BF(0))
        gm = jnp.where(on, gp, BF(0))
        probs = jnp.exp(dg(kp, qm, NT) - log[p, h : h + 1, :])
        gv += dg(probs.astype(BF), gm, NN)
        grad_probs = dg(vp, gm, NT)
        inner = jnp.sum(probs * grad_probs, axis=0, keepdims=True)
        grad_scores = (probs * (grad_probs - inner)).astype(BF)
        gk += dg(grad_scores, qm, NN)
        gq += dg(grad_scores, km, TN)
    q[:, cols] = gq.astype(BF)
    k[:, cols] = gk.astype(BF)
    v[:, cols] = gv.astype(BF)


N_OWN = 9
N_PART = 8
LATE = ()
ORDER = [
    ("Z", 0), ("F", 0), ("S", 0), ("Z", 1), ("T", 0), ("D", 0), ("Z", 2), ("F", 1), ("S", 1), ("Z", 3),
    ("F", 2), ("S", 2), ("Z", 4), ("F", 3), ("T", 1), ("D", 1), ("S", 3), ("F", 4), ("Z", 5), ("T", 2),
    ("D", 2), ("S", 4), ("F", 5), ("Z", 6), ("T", 3), ("D", 3), ("T", 4), ("F", 6), ("D", 4), ("Z", 7),
    ("S", 5), ("F", 7), ("T", 5), ("Z", 8), ("D", 5), ("S", 6), ("F", 8), ("T", 6), ("s", 0), ("S", 7),
    ("D", 6), ("T", 7), ("S", 8), ("s", 1), ("D", 7), ("T", 8), ("D", 8), ("a", 0), ("b", 0), ("a", 1),
    ("e", 0), ("b", 1), ("e", 1), ("a", 2), ("b", 2), ("f", 0), ("f", 1), ("e", 2), ("a", 3), ("b", 3),
    ("a", 4), ("f", 2), ("e", 3), ("b", 4), ("e", 4), ("a", 5), ("a", 6), ("a", 7), ("b", 5), ("f", 3),
    ("e", 5), ("f", 4), ("b", 6), ("b", 7), ("f", 5), ("e", 6), ("e", 7), ("f", 6), ("f", 7),
]
PUMPS = {
    "half": (1, 3),
    "LN1": 1,
    "q": (0, 0, 0, 1),
    "k": (0, 0, 0, 1),
    "v": (0, 0, 0, 0),
    "att": (1, 0, 2, 2, 0, 0, 0, 0),
    "out": 0,
    "LN2": 3,
    "up": ((0, 1, 0, 0), (0, 0, 0, 1)),
    "dn": ((0, 1, 0, 1), (0, 0, 0, 1)),
    "grad": (3, 3, 2, 1, 2),
    "up_back": ((0, 1), (0, 1)),
    "LN2_back": 1,
    "att_back": (0, 2, 1, 0, 2, 2, 0, 1),
    "qk_back": (2, 0, 2, 1),
    "v_back": (0, 0),
    "LN1_back": 3,
    "swap": (1, 0, 0),
}


def block_kernel(zs, tokens_in, cot, mask, *refs):
    n, parts = N_OWN, N_PART
    refs = list(refs)

    def take(count):
        got = refs[:count]
        del refs[:count]
        return got if count > 1 else got[0]

    biases, vectors = take(3), take(6)
    wq, wk, wv, wo, wu, wd = take(6)
    block_out, tokens_grad, gq_out, gk_out, gv_out, go_out, gu_out, gd_out, small_out = take(9)
    bufs, rs, rz = take(n), take(4), take(parts)
    weights = bufs[1:]
    own = take(n)
    kept, rf = take(parts), take(parts)
    rs = rs + take(4)
    (send, stage, wt, pair, grad_out, attn_in, q, k, v, log, mixed, middle, mlp_in, hidden, grad_pre, acc) = take(16)
    vstage, vecs, dvec, dsum, pad, long, slab, small, small_in = take(9)
    load_sem, wt_sem, vsend, vrecv = take(4)
    gsems, ssems = take(11), take(7)
    tokens, grad_mixed, grad_attn = pair.at[0], pair.at[0], pair.at[1]
    rows, dim = attn_in.shape
    hw = wq.shape[1]
    half = wu.shape[1] // 2
    at = coords(zs)
    c = at["c"]
    g = Gather(at, own, bufs, LATE, gsems)
    s = Scatter(at, kept, rs, rf, rz, stage, range(4, parts), ssems)
    w_q, w_k, w_v, w_o, w_u0, w_u1, w_d0, w_d1 = weights

    enter(at)
    load_tokens = pltpu.make_async_copy(tokens_in, tokens, load_sem.at[0])
    load_cot = pltpu.make_async_copy(cot, grad_out, load_sem.at[1])
    load_tokens.start()
    load_cot.start()
    place_vectors(at, biases, vectors, own[0], pad, long, slab)
    own[1][...] = wq[...].astype(BF)
    own[2][...] = wk[...].astype(BF)
    entered(at)

    for i in range(3):
        g.start_z(i)
        g.start_own(i)
    own[3][...] = wv[...].astype(BF)
    own[4][...] = wo[...].T.astype(BF)
    g.start_own(3)
    g.start_own(4)
    own[5][...] = wu[:, :half].astype(BF)
    own[6][...] = wu[:, half:].astype(BF)
    own[7][...] = wd[:half, :].T.astype(BF)
    own[8][...] = wd[half:, :].T.astype(BF)

    def after_z(i):
        if i + 2 < n and i > 0:
            g.start_z(i + 2)
            if i + 2 >= 5:
                g.start_own(i + 2)
        g.after_z(i)

    def finish_part(i):
        sums = s.total(i)
        if i < 2:
            gd_out[i * half : (i + 1) * half, :] = sums.T
        elif i < 4:
            gu_out[:, (i - 2) * half : (i - 1) * half] = sums
        elif i == 4:
            go_out[...] = sums.T
        else:
            (gv_out, gq_out, gk_out)[i - 5][...] = sums

    kinds = {
        "X": g.pass_z, "Z": after_z, "F": g.after_first, "S": g.after_second, "T": g.after_across, "D": g.done,
        "s": s.start, "a": s.pass_on, "b": s.after_second, "e": s.after_first, "f": finish_part,
    }
    steps = list(reversed(ORDER))

    def take_step():
        what, i = steps.pop()
        kinds[what](i)

    def pump(count=1):
        for _ in range(min(count, len(steps))):
            take_step()

    def until(what, i):
        while (what, i) in steps:
            take_step()

    def tile_copy(w, t, side=0, part=0):
        width = w.shape[-1]
        dst = wt.at[t, :, :, :, pl.ds(side * hw, width)]
        return pltpu.make_async_copy(w.at[t // 2, t % 2], dst, wt_sem.at[part, t])

    def fetch(w, side=0, part=0):
        for t in range(4):
            tile_copy(w, t, side, part).start()

    def tile(w, t, side=0, part=0):
        tile_copy(w, t, side, part).wait()
        return wt[t, :, :, :, side * hw : side * hw + w.shape[-1]].reshape(dim, -1)

    def tiles(w, pumps, body):
        spans(pumps, pump, lambda t: body(t, tile(w, t)))

    def columns(t):
        return pl.ds(pl.multiple_of(t * hw, hw), hw)

    def product(i, make):
        slot = i % 2
        width = kept[i].shape[-1]

        def out(x):
            return send.at[slot, x, :, :, :, pl.ds(0, width)]

        if i >= 2:
            for x in range(2):
                before = send.at[slot, x, :, :, :, pl.ds(0, kept[i - 2].shape[-1])]
                s.to_sibling(i - 2, x, before).wait_send()

        @pl.loop(0, 2)
        def _(x):
            send[slot, x, :, :, :, :width] = make(2 * x + 1 - c).astype(BF).reshape(kept[i].shape[1:])
            s.to_sibling(i, x, out(x)).start()

        @pl.loop(0, 2)
        def _(x):
            terms = make(2 * x + c)
            s.to_sibling(i, x, out(x)).wait_recv()
            other = kept[i][x].reshape(dim, -1).astype(F32)
            kept[i][x] = (terms + other).astype(BF).reshape(kept[i].shape[1:])

        if i >= 2:
            s.start(i)
        pump(PUMPS["grad"][i])

    until("D", 0)
    for t in range(4):
        fetch_vectors = pltpu.make_async_copy(bufs[0].at[t // 2, t % 2], vstage, load_sem.at[2])
        fetch_vectors.start()
        fetch_vectors.wait()
        vecs[t] = jnp.sum(vstage[...].astype(F32).reshape(-1, 16, 256), axis=0)
    for t in range(3):
        for which in range(2):
            first = 6 + 4 * which
            dvec[2 * t + which : 2 * t + which + 1, :] = jnp.concatenate(
                [vecs[t, first + i : first + i + 1, :] for i in range(4)], axis=1
            )
    keep = mask[at["tn"]].astype(F32)
    load_tokens.wait()
    load_cot.wait()

    def norm_a(sl):
        grad_out[sl, :] = (grad_out[sl, :].astype(F32) * keep).astype(BF)
        normed, _ = norm_parts(tokens[sl, :].astype(F32))
        attn_in[sl, :] = (normed * dvec[0:1, :] + dvec[1:2, :]).astype(BF)

    by_rows(rows, norm_a)
    pump(PUMPS["LN1"])

    def project(dst, bias_row):
        def body(t, w):
            got = dg(attn_in[...], w, NN)
            if bias_row is not None:
                got = got + vecs[t, bias_row : bias_row + 1, :]
            dst[:, columns(t)] = got.astype(BF)

        return body

    for i, (w, dst, bias_row, name) in enumerate(((w_q, q, 0, "q"), (w_k, k, None, "k"), (w_v, v, 1, "v"))):
        until("D", 1 + i)
        fetch(w)
        tiles(w, PUMPS[name], project(dst, bias_row))
    spans(PUMPS["att"], pump, lambda p: attend_pair(p, q, k, v, mixed, log))
    until("D", 4)
    fetch(w_o)
    acc[...] = jnp.zeros_like(acc)

    def out_project(i):
        two = [dg(mixed[:, columns(t)], tile(w_o, t), NT) for t in (2 * i, 2 * i + 1)]
        acc[...] += two[0] + two[1]

    spans((0, PUMPS["out"]), pump, out_project)

    def norm_m(sl):
        mid = tokens[sl, :].astype(F32) + acc[sl, :] + dvec[4:5, :]
        middle[sl, :] = mid
        normed, _ = norm_parts(mid)
        mlp_in[sl, :] = (normed * dvec[2:3, :] + dvec[3:4, :]).astype(BF)

    by_rows(rows, norm_m)
    pump(PUMPS["LN2"])

    def hidden_of(which, t):
        if which == 0:
            return hidden.at[t]
        return pair.at[t // 2, :, pl.ds(pl.multiple_of(t % 2 * half, half), half)]

    def up(which):
        def body(t, w):
            bias = jnp.concatenate(
                [vecs[t, 2 + 2 * which + i : 3 + 2 * which + i, :] for i in range(2)], axis=1
            )
            pre = dg(mlp_in[...], w, NN) + bias
            sigma = 0.5 + 0.5 * jnp.tanh((0.5 * SLOPE) * pre)
            hid = pre * sigma
            hidden_of(which, t)[...] = hid.astype(BF)
            grad_pre[which * 4 + t] = (sigma + SLOPE * hid * (1.0 - sigma)).astype(BF)

        return body

    for which, w in enumerate((w_u0, w_u1)):
        until("D", 5 + which)
        fetch(w)
        tiles(w, PUMPS["up"][which], up(which))
        if which == 0:
            product(0, lambda t: dg(grad_out[...], hidden_of(0, t)[...], TN))
    product(1, lambda t: dg(grad_out[...], hidden_of(1, t)[...], TN))
    acc[...] = jnp.zeros_like(acc)

    def down(which):
        def body(t, w):
            j = which * 4 + t
            acc[...] += dg(hidden_of(which, t)[...], w, NT)
            grad_hidden = dg(grad_out[...], w, NN)
            grad_pre[j] = (grad_hidden * grad_pre[j].astype(F32)).astype(BF)

        return body

    def up_terms(which):
        return lambda t: dg(mlp_in[...], grad_pre[which * 4 + t], TN)

    until("D", 7)
    fetch(w_d0)
    tiles(w_d0, PUMPS["dn"][0], down(0))
    product(2, up_terms(0))
    until("D", 8)
    fetch(w_d1)
    tiles(w_d1, PUMPS["dn"][1], down(1))
    fetch(w_u0)

    def finish_rows(sl):
        pair[0, sl, :] = ((middle[sl, :] + acc[sl, :] + dvec[5:6, :]) * keep).astype(BF)

    by_rows(rows, finish_rows)
    store_block = pltpu.make_async_copy(pair.at[0], block_out, load_sem.at[2])
    store_block.start()

    product(3, up_terms(1))

    def up_back(which):
        def body(i):
            w = w_u1 if which else w_u0
            two = [dg(grad_pre[which * 4 + t], tile(w, t), NT) for t in (2 * i, 2 * i + 1)]
            acc[...] += two[0] + two[1]

        return body

    acc[...] = jnp.zeros_like(acc)
    spans(PUMPS["up_back"][0], pump, up_back(0))
    fetch(w_u1)
    spans(PUMPS["up_back"][1], pump, up_back(1))
    fetch(w_o)
    dsum[...] = jnp.zeros_like(dsum)

    def norm_back(values, grad, gain, at_row):
        normed, inverse = norm_parts(values)
        scaled = grad * gain
        dsum[at_row : at_row + 1, :] += jnp.sum(grad * normed, axis=0, keepdims=True)
        dsum[at_row + 1 : at_row + 2, :] += jnp.sum(grad, axis=0, keepdims=True)
        return inverse * (
            scaled
            - jnp.mean(scaled, axis=-1, keepdims=True)
            - normed * jnp.mean(scaled * normed, axis=-1, keepdims=True)
        )

    def norm_m_back(sl):
        through = grad_out[sl, :].astype(F32)
        grad = through + norm_back(middle[sl, :], acc[sl, :], dvec[2:3, :], 2)
        dsum[4:5, :] += jnp.sum(grad, axis=0, keepdims=True)
        dsum[5:6, :] += jnp.sum(through, axis=0, keepdims=True)
        middle[sl, :] = grad
        grad_attn[sl, :] = grad.astype(BF)

    by_rows(rows, norm_m_back)
    store_block.wait()
    pump(PUMPS["LN2_back"])

    def mixed_back(t, w):
        grad_mixed[:, columns(t)] = dg(grad_attn[...], w, NN).astype(BF)

    tiles(w_o, (0, 0, 0, 0), mixed_back)
    product(4, lambda t: dg(grad_attn[...], mixed[:, columns(t)], TN))
    fetch(w_q, 0, 0)
    fetch(w_k, 1, 1)

    def half_products(xh, last):
        todo = []
        for i, grad, side in ((5, v, 0), (6, q, 0), (7, k, 1)):
            out = send.at[i % 2, xh, :, :, :, pl.ds(side * hw, hw)]
            todo.append((i, grad, out))
            if i < 7:
                before = send.at[i % 2, xh, :, :, :, pl.ds(0, kept[i - 2].shape[-1])]
                s.to_sibling(i - 2, xh, before).wait_send()
            t = 2 * xh + 1 - c
            out[...] = dg(attn_in[...], grad[:, columns(t)], TN).astype(BF).reshape(kept[i].shape[1:])
            s.to_sibling(i, xh, out).start()
        for i, grad, out in todo:
            terms = dg(attn_in[...], grad[:, columns(2 * xh + c)], TN)
            s.to_sibling(i, xh, out).wait_recv()
            other = kept[i][xh].reshape(dim, -1).astype(F32)
            kept[i][xh] = (terms + other).astype(BF).reshape(kept[i].shape[1:])
            if not last:
                s.to_second(i, 1).start()

            @pl.when(c == (1 if last else 0))
            def _():
                s.to_second(i, 0).start()

    pairs = dim // (4 * HD)
    other_x = 1 - at["x"]
    for last, xh in enumerate((other_x, at["x"])):
        spans(
            PUMPS["att_back"][last * pairs : (last + 1) * pairs],
            pump,
            lambda p, xh=xh: attend_pair_back(xh * pairs + p, q, k, v, grad_mixed, log),
        )
        half_products(xh, last)
        pump(PUMPS["half"][last])
    reload_tokens = pltpu.make_async_copy(tokens_in, tokens, load_sem.at[0])
    reload_tokens.start()
    for t in range(4):
        cols = slice(t * hw, (t + 1) * hw)
        small[t, 0:1, :] = jnp.sum(q[:, cols].astype(F32), axis=0, keepdims=True)
        small[t, 1:2, :] = jnp.sum(v[:, cols].astype(F32), axis=0, keepdims=True)
        for which in range(2):
            sums = jnp.sum(grad_pre[which * 4 + t].astype(F32), axis=0, keepdims=True)
            for i in range(2):
                row = 2 + 2 * which + i
                small[t, row : row + 1, :] = sums[:, i * 256 : (i + 1) * 256]
        small[t, 6:16, :] = jnp.zeros((10, 256), F32)
    acc[...] = jnp.zeros_like(acc)

    def qk_back(t):
        tile_copy(w_q, t, 0, 0).wait()
        tile_copy(w_k, t, 1, 1).wait()
        both = jnp.concatenate([q[:, columns(t)], k[:, columns(t)]], axis=1)
        acc[...] += dg(both, wt[t].reshape(dim, -1), NT)

    spans(PUMPS["qk_back"], pump, qk_back)
    fetch(w_v)

    def v_back(i):
        two = [dg(v[:, columns(t)], tile(w_v, t), NT) for t in (2 * i, 2 * i + 1)]
        acc[...] += two[0] + two[1]

    spans(PUMPS["v_back"], pump, v_back)
    reload_tokens.wait()

    def norm_a_back(sl):
        values = tokens[sl, :].astype(F32)
        middle[sl, :] += norm_back(values, acc[sl, :], dvec[0:1, :], 0)

    by_rows(rows, norm_a_back)
    store_grad = pltpu.make_async_copy(middle, tokens_grad, load_sem.at[1])
    store_grad.start()
    pump(PUMPS["LN1_back"])
    for i in range(6):
        for j in range(4):
            row = 6 + 4 * (i % 2) + j
            small[i // 2, row : row + 1, :] = dsum[i : i + 1, j * 256 : (j + 1) * 256]
    x, y = at["x"], at["y"]
    peers = [at["sibling"], (at["dp"], at["tn"] + 2 - 4 * x), (at["dp"] + 1 - 2 * y, at["tn"])]

    def swap(i):
        return remote(small, small_in.at[i], vsend.at[i], vrecv.at[i], peers[i])

    def swap_z(step):
        return remote(small, small_in.at[2 + step], vsend.at[2 + step], vrecv.at[2 + step], z_peer(at, step))

    for i in range(3):
        swap(i).start()
        pump(PUMPS["swap"][i])
        swap(i).wait()
        small[...] += small_in[i]

    @pl.loop(1, zs)
    def _(step):
        swap_z(step).start()

    pump(len(steps))

    @pl.loop(1, zs)
    def _(step):
        swap_z(step).wait()

    small_out[...] = lax.fori_loop(1, zs, lambda step, sums: sums + small_in[2 + step], small[...])
    store_grad.wait()
    for i in range(n):
        g.drain(i)
    for i in range(parts):
        if i >= parts - 3:
            for x_ in range(2):
                out = send.at[i % 2, x_, :, :, :, pl.ds((i == 7) * hw, hw)]
                s.to_sibling(i, x_, out).wait_send()
        s.drain(i)


def block(tokens, cot, mask, biases, vectors, weights, zs):
    rows, dim = tokens.shape
    wq, wk, wv, wo, wu, wd = weights
    r, hw = wq.shape
    half = wu.shape[1] // 2
    n, parts = N_OWN, N_PART
    vmem, hbm = pl.BlockSpec(memory_space=pltpu.VMEM), pl.BlockSpec(memory_space=pl.ANY)
    shape, sem = jax.ShapeDtypeStruct, pltpu.SemaphoreType.DMA
    own_widths = [hw] * 4 + [half] * 4
    widths = [half] * 4 + [hw] * 4
    outs = [
        shape((rows, dim), BF),
        shape((rows, dim), F32),
        shape((r, hw), F32),
        shape((r, hw), F32),
        shape((r, hw), F32),
        shape((hw, r), F32),
        shape((r, 2 * half), F32),
        shape((2 * half, r), F32),
        shape((4, 16, 256), F32),
    ]
    outs += [shape((2, 2, zs, 2, 16, 256), BF)]
    outs += [shape((2, 2, zs, 2, r, w), BF) for w in own_widths]
    outs += [shape((2, zs, r, w), BF) for w in widths[:4]]
    outs += [shape((zs - 1, r, w), BF) for w in widths]
    act, wide = pltpu.VMEM((rows, dim), BF), pltpu.VMEM((rows, dim), F32)
    return pl.pallas_call(
        functools.partial(block_kernel, zs),
        out_shape=outs,
        in_specs=[hbm, hbm, pl.BlockSpec(memory_space=pltpu.SMEM)] + [vmem] * 15,
        out_specs=[hbm] * 2 + [vmem] * 7 + [hbm] * (n + 4 + parts),
        scratch_shapes=[pltpu.VMEM((16, 256), BF)]
        + [pltpu.VMEM((r, w), BF) for w in own_widths]
        + [pltpu.VMEM((2, zs, 2, r, w), BF) for w in widths]
        + [pltpu.VMEM((zs, r, w), BF) for w in widths]
        + [pltpu.VMEM((2, zs, r, w), BF) for w in widths[4:]]
        + [
            pltpu.VMEM((2, 2, zs, 2, r, half), BF),
            pltpu.VMEM((zs, r, half), BF),
            pltpu.VMEM((4, zs, 2, r, half), BF),
            pltpu.VMEM((2, rows, dim), BF),
            act,
            act,
            act,
            act,
            act,
            pltpu.VMEM((dim // HD // 2, 2, rows), F32),
            act,
            wide,
            act,
            pltpu.VMEM((4, rows, half), BF),
            pltpu.VMEM((8, rows, half), BF),
            wide,
            pltpu.VMEM((zs, 2, 16, 256), BF),
            pltpu.VMEM((4, 16, 256), F32),
            pltpu.VMEM((8, dim), F32),
            pltpu.VMEM((8, dim), F32),
            pltpu.VMEM((8, 256), F32),
            pltpu.VMEM((8, dim), F32),
            pltpu.VMEM((16, 256), F32),
            pltpu.VMEM((4, 16, 256), F32),
            pltpu.VMEM((2 + zs, 4, 16, 256), F32),
            sem((3,)),
            sem((2, 4)),
            sem((2 + zs,)),
            sem((2 + zs,)),
            sem((n,)),
        ]
        + [sem((n, zs))] * 6
        + [sem((n, 5))] * 2
        + [sem((n, zs))] * 2
        + [sem((parts, 2))] * 2
        + [sem((parts, 3))] * 2
        + [sem((parts, zs))] * 2
        + [sem((1,))],
        compiler_params=pltpu.CompilerParams(
            collective_id=0, has_side_effects=True, vmem_limit_bytes=62 * 1024 * 1024
        ),
        name="block",
    )(tokens, cot, mask, *biases, *vectors, *weights)[:9]


def finish_kernel(n, *refs):
    big, sums, big_out, refs = refs[:n], refs[n], refs[n + 1 : 2 * n + 1], refs[2 * n + 1 :]
    biases, vectors, held, (in_sem, out_sem) = refs[:3], refs[3:9], refs[9 : 9 + n], refs[9 + n :]
    reads = [pltpu.make_async_copy(big[i], held[i], in_sem.at[i]) for i in range(n)]
    copies = [pltpu.make_async_copy(held[i], big_out[i], out_sem.at[i]) for i in range(n)]
    for read in reads:
        read.start()
    for read, copy in zip(reads, copies):
        read.wait()
        copy.start()
    dp, tn = lax.axis_index("dp"), lax.axis_index("tensor")
    here = sums[tn]

    def at_lane(rows, lane):
        return pltpu.roll(rows, lax.rem(256 - lane, 256), 1)

    heads, w = biases[0].shape
    for h in range(heads):
        moved = at_lane(here, h * HD + dp * w)
        biases[0][h : h + 1, :] = moved[0:1, :w]
        biases[1][h : h + 1, :] = moved[1:2, :w]
    w = biases[2].shape[1]
    for odd in range(2):
        moved = at_lane(here, 128 * odd + dp * w)
        for i in range(4):
            biases[2][2 * i + odd : 2 * i + odd + 1, :] = moved[2 + i : 3 + i, :w]
    for i in range(6):
        w = vectors[i].shape[1]
        slab = sums[i // 2]
        lane = dp * w
        first = 6 + 4 * (i % 2)
        moved = at_lane(slab, lane % 256)
        rows = lax.broadcasted_iota(jnp.int32, moved.shape, 0)
        row = jnp.sum(jnp.where(rows == first + lane // 256, moved, 0.0), axis=0, keepdims=True)
        vectors[i][...] = row[:, :w]
    for copy in copies:
        copy.wait()


def finish(big, sums, like):
    n = len(big)
    vmem, hbm = pl.BlockSpec(memory_space=pltpu.VMEM), pl.BlockSpec(memory_space=pl.ANY)
    return pl.pallas_call(
        functools.partial(finish_kernel, n),
        out_shape=[jax.ShapeDtypeStruct(a.shape, a.dtype) for a in (*big, *like)],
        in_specs=[hbm] * n + [vmem],
        out_specs=[hbm] * n + [vmem] * len(like),
        scratch_shapes=[pltpu.VMEM(a.shape, a.dtype) for a in big] + [pltpu.SemaphoreType.DMA((n,))] * 2,
        name="finish",
    )(*big, sums)


def on_device(
    tokens,
    cotangent,
    image_mask,
    query_weight,
    key_weight,
    value_weight,
    out_weight,
    up_weight,
    down_weight,
    query_bias,
    value_bias,
    up_bias,
    attn_gain,
    attn_shift,
    mlp_gain,
    mlp_shift,
    out_bias,
    down_bias,
):
    zs = lax.axis_size("dp") // 2
    biases = (query_bias, value_bias, up_bias)
    vectors = tuple(v.reshape(1, -1) for v in (attn_gain, attn_shift, mlp_gain, mlp_shift, out_bias, down_bias))
    weights = (query_weight, key_weight, value_weight, out_weight, up_weight, down_weight)
    *grads, sums = block(tokens, cotangent, image_mask, biases, vectors, weights, zs)
    done = finish(grads, sums, biases + vectors)
    return tuple(done[:11]) + tuple(v.reshape(-1) for v in done[11:])


def solution(mesh):
    wide, tall = P("dp", "tensor"), P("tensor", "dp")
    rows = P(("dp", "tensor"), None)
    weights = (wide, wide, wide, tall, wide, tall, tall, tall, tall)
    vectors = (P("dp"),) * 6
    return jax.shard_map(
        on_device,
        mesh=mesh,
        in_specs=(rows, rows, P("dp")) + weights + vectors,
        out_specs=(rows, rows) + weights + vectors,
        check_vma=False,
    )
```
